512 devices in a mesh: rows: 128 (over y, z, core), cols: 4 (over x).
Axes of the slice: x: 4, y: 8, z: 8, core: 2. Of those that a mesh axis runs over, the one named last changes fastest.
Arguments:
- gradient: float32 [8192, 29568], P('rows', 'cols'), as said below
- start_block: float32 [29568, 64], P('cols'), may hold values from -0.03125 to 0.03125
- activations: float32 [8192, 29568], P('rows', 'cols'), may hold values from -6 to 6
- out_grads: float32 [8192, 8192], P('rows', 'cols'), may hold values from -6 to 6
Outputs:
- left_factor: float32 [8192, 64], P('rows')
- right_factor: float32 [29568, 64], P('cols')
- scores: float32 [8192], P('rows')
The draws below stay inside these ranges and needn't reach their ends.
Inputs may be any that keep to these rules, and one draw needn't show every extreme that they name: real-valued gradient entries, of order 29568 ** -0.5.
All inputs are finite; a program needn't handle non-finite values.
Results may differ from the reference program's by a relative error of at most 0.00013.
Values sent between devices are 32-bit elements; how exact they have to be, the bound alone decides.
No kernel may reach another device: no remote copies, remote signals or barrier semaphores. Data moves between devices by JAX's collectives and lax.ppermute only.
A program may use at most 64 MiB of HBM per device.

```python
import jax
import jax.numpy as jnp
from jax import lax

M = 8192
N = 29568
R = 64
ITERS = 2
TOKENS = 8192


def draw_gradient(key, part):
    first, second, third = jax.random.split(jax.random.fold_in(key, 7), 3)
    base = jnp.clip(jax.random.normal(first, (M, N), jnp.float32), -6.0, 6.0)
    upper = 10.0
    rising = 3.0 ** (jnp.arange(M, dtype=jnp.float32) / M)
    row_scale = jnp.exp(jax.random.uniform(second, (M,), jnp.float32) * jnp.log(upper)) * rising
    col_scale = jnp.exp(jax.random.uniform(third, (N,), jnp.float32) * jnp.log(upper))
    return base * row_scale[:, None] * col_scale[None, :] / (40.0 * jnp.sqrt(jnp.float32(N)))


def steps_of(stream_key, dims, pieces, smallest, high):
    level, own = 1.0, jax.random.fold_in(stream_key, 6)
    for axis_at, blocks in pieces:
        heights = jnp.exp(jax.random.uniform(jax.random.fold_in(own, axis_at), (blocks,), jnp.float32, smallest / len(pieces), high / len(pieces)))
        level = level * jnp.repeat(heights, dims[axis_at] // blocks).reshape([-1 if axis == axis_at else 1 for axis in range(len(dims))])
    return level


def scatter_about(key, shape, deviation, limit, cuts=(), held_as=jnp.bfloat16):
    array = deviation * jax.random.normal(key, shape, jnp.float32)
    if cuts:
        array = array * steps_of(key, shape, cuts, -0.22, 0.18)
    return jnp.clip(array, -limit, limit).astype(held_as)


def setup_inputs(seed: int = 0) -> dict:
    key_of = jax.random.split(jax.random.key(seed), 5)
    return {
        "gradient": draw_gradient(jax.random.fold_in(key_of[4], 71), 0),
        "start_block": scatter_about(key_of[1], (N, R), N ** -0.5, 0.03125, ((0, 4),), jnp.float32),
        "activations": scatter_about(key_of[2], (TOKENS, N), 1.0, 6.0, ((0, 128), (1, 4)), jnp.float32),
        "out_grads": scatter_about(key_of[3], (TOKENS, M), 1.0, 6.0, ((0, 128), (1, 4)), jnp.float32),
    }


HIGH = lax.Precision.HIGHEST

def cholqr(block):
    gram = jnp.dot(block.T.astype(jnp.float32), block.astype(jnp.float32), precision=HIGH, preferred_element_type=jnp.float32)
    lower = jnp.linalg.cholesky(gram)
    return lax.linalg.triangular_solve(lower, block, left_side=False, lower=True, transpose_a=True)

def reference(gradient, start_block, activations, out_grads):
    omega = start_block
    for step in range(ITERS):
        ysum = jnp.dot(gradient.astype(jnp.float32), omega.astype(jnp.float32), precision=HIGH, preferred_element_type=jnp.float32)
        left = cholqr(ysum)
        zsum = jnp.dot(gradient.T.astype(jnp.float32), left.astype(jnp.float32), precision=HIGH, preferred_element_type=jnp.float32)
        right = cholqr(zsum)
        omega = right
    core = jnp.dot(left.T.astype(jnp.float32), jnp.dot(gradient.astype(jnp.float32), right.astype(jnp.float32), precision=HIGH, preferred_element_type=jnp.float32).astype(jnp.float32), precision=HIGH, preferred_element_type=jnp.float32)
    token_left = jnp.dot(out_grads.astype(jnp.float32), left.astype(jnp.float32), precision=HIGH, preferred_element_type=jnp.float32)
    token_right = jnp.dot(activations.astype(jnp.float32), right.astype(jnp.float32), precision=HIGH, preferred_element_type=jnp.float32)
    mixed = jnp.dot(token_left.astype(jnp.float32), core.astype(jnp.float32), precision=HIGH, preferred_element_type=jnp.float32)
    scores = jnp.sum(mixed * token_right, axis=1)
    return (left, right, scores)
```

```python
import functools

import jax
import jax.numpy as jnp
from jax import lax
from jax.experimental import pallas as pl
from jax.experimental.pallas import tpu as pltpu
from jax.sharding import Mesh
from jax.sharding import PartitionSpec as P

ITERS = 2
R = 64
H = R // 2
LANES = 128
F32 = jnp.float32
ROWS = ("y", "z", "c")
CHIPS = ("y", "z")
PEERS = ("c", "x")
HIGH = lax.Precision.HIGHEST

VMEM = pl.BlockSpec(memory_space=pltpu.VMEM)
SMEM = pl.BlockSpec(memory_space=pltpu.SMEM)


def nn(a, b):
    return lax.dot_general(a, b, (((1,), (0,)), ((), ())), precision=HIGH, preferred_element_type=F32)


def nt(a, b):
    return lax.dot_general(a, b, (((1,), (1,)), ((), ())), precision=HIGH, preferred_element_type=F32)


def call(body, out_shape, n_in, scalars=0, scratch=()):
    specs = [SMEM] * scalars + [VMEM] * (n_in - scalars)
    outs = jax.tree.map(lambda _: VMEM, out_shape)
    return pl.pallas_call(
        body,
        out_shape=out_shape,
        in_specs=specs,
        out_specs=outs,
        scratch_shapes=list(scratch),
        compiler_params=pltpu.CompilerParams(vmem_limit_bytes=48 * 2**20),
    )


def shape(*dims):
    return jax.ShapeDtypeStruct(dims, F32)


def rsqrt(s):
    t = lax.rsqrt(s)
    return t * (1.5 - 0.5 * s * t * t)


def fold(square):
    return jnp.concatenate([square[:H], square[H:]], axis=1)


def unfold(half):
    return jnp.concatenate([half[:, :R], half[:, R:]], axis=0)


def factor(gram, rows_ref):
    b = 4
    line = lax.broadcasted_iota(jnp.int32, (R, R), 0)
    lane = lax.broadcasted_iota(jnp.int32, (R, R), 1)
    both = jnp.concatenate([gram, (line == lane).astype(F32)], axis=1)
    groups = [both[8 * g : 8 * g + 8] for g in range(R // 8)]
    sub = lax.broadcasted_iota(jnp.int32, (8, LANES), 0)
    for k in range(0, R, b):
        g0, off = divmod(k, 8)
        rows = [jnp.broadcast_to(groups[g0][off + i : off + i + 1], (8, LANES)) for i in range(b)]
        live = range(g0 if off + b < 8 else g0 + 1, R // 8)
        cols = {
            g: [jnp.broadcast_to(groups[g][:, k + j : k + j + 1], (8, LANES)) for j in range(b)]
            for g in live
        }
        low = [[None] * b for _ in range(b)]
        inv = [None] * b
        for i in range(b):
            splat = [jnp.broadcast_to(rows[i][:, k + j : k + j + 1], (8, LANES)) for j in range(i + 1)]
            for j in range(i):
                s = splat[j]
                for q in range(j):
                    s = s - low[i][q] * low[j][q]
                low[i][j] = s * inv[j]
            d = splat[i]
            for q in range(i):
                d = d - low[i][q] * low[i][q]
            inv[i] = rsqrt(d)

        def solved(lines):
            done = []
            for i in range(b):
                s = lines[i]
                for q in range(i):
                    s = s - low[i][q] * done[q]
                done.append(s * inv[i])
            return done

        new_rows = solved(rows)
        for i in range(b):
            rows_ref[k + i : k + i + 1, :] = new_rows[i][0:1]
        for g in live:
            f = solved(cols[g])
            upd = f[0] * new_rows[0]
            for i in range(1, b):
                upd = upd + f[i] * new_rows[i]
            if g == g0:
                upd = jnp.where(sub >= off + b, upd, 0.0)
            groups[g] = groups[g] - upd


def inverse_of(rows_ref):
    line = lax.broadcasted_iota(jnp.int32, (R, R), 0)
    lane = lax.broadcasted_iota(jnp.int32, (R, R), 1)
    return jnp.where(line >= lane, rows_ref[:, R:], 0.0)


def lower_t_of(rows_ref):
    line = lax.broadcasted_iota(jnp.int32, (R, R), 0)
    lane = lax.broadcasted_iota(jnp.int32, (R, R), 1)
    return jnp.where(line <= lane, rows_ref[:, :R], 0.0)


def halves_body(c_ref, a_ref, keep_ref, send_ref):
    width = keep_ref.shape[1]
    rest = a_ref.shape[1] - width

    @pl.when(c_ref[0] == 0)
    def _():
        keep_ref[...] = a_ref[:, :width]
        send_ref[...] = jnp.zeros_like(send_ref)
        send_ref[:, :rest] = a_ref[:, width:]

    @pl.when(c_ref[0] != 0)
    def _():
        send_ref[...] = a_ref[:, :width]
        keep_ref[...] = jnp.zeros_like(keep_ref)
        keep_ref[:, :rest] = a_ref[:, width:]


def swapped(core, a, width):
    lines = a.shape[0]
    keep, send = call(halves_body, (shape(lines, width), shape(lines, width)), 2, scalars=1)(core, a)
    got = lax.ppermute(send, "c", [(0, 1), (1, 0)])
    return keep, got


def first_body(g_ref, o_ref, out_ref):
    y = fold(nn(g_ref[...], o_ref[...]).T)
    for i in range(out_ref.shape[0]):
        out_ref[i] = y


def put_slots(yt, g_refs, core, out_ref):
    mine, other = g_refs[0][...], g_refs[1][...]
    low = yt[:, :R]
    high = yt[:, R:]
    a = jnp.where(core == 0, low, high)
    b = jnp.where(core == 0, high, low)
    z = nn(a, mine) + nn(b, other)
    tiles = z.shape[1] // LANES
    for t in range(tiles):
        part = z[:, t * LANES : (t + 1) * LANES]
        out_ref[2 * t] = part[:H]
        out_ref[2 * t + 1] = part[H:]
    out_ref[2 * tiles] = fold(nt(yt, yt))
    for s in range(2 * tiles + 1, out_ref.shape[0]):
        out_ref[s] = jnp.zeros((H, LANES), F32)


def spread_first_body(c_ref, got_ref, g_ref, h_ref, out_ref):
    n = got_ref.shape[0] // 2
    parts = []
    for c in range(2):
        s = got_ref[c * n]
        for i in range(1, n):
            s = s + got_ref[c * n + i]
        parts.append(unfold(s))
    yt = jnp.concatenate(parts, axis=1)
    put_slots(yt, (g_ref, h_ref), c_ref[0], out_ref)


def spread_body(c_ref, got_ref, g_ref, h_ref, out_ref, yt_ref, rows_ref):
    s = got_ref[0]
    for i in range(1, got_ref.shape[0]):
        s = s + got_ref[i]
    factor(unfold(s[R:]), rows_ref)
    yt = nn(inverse_of(rows_ref), s[:R])
    yt_ref[...] = yt
    put_slots(yt, (g_ref, h_ref), c_ref[0], out_ref)


def total_body(got_ref, out_ref):
    n = got_ref.shape[0]
    s = got_ref[0]
    for i in range(1, n):
        s = s + got_ref[i]
    for i in range(n):
        out_ref[i] = s


def total_with_body(got_ref, more_ref, out_ref):
    n = got_ref.shape[0]
    s = got_ref[0]
    for i in range(1, n):
        s = s + got_ref[i]
    more = more_ref[...]
    for i in range(n):
        out_ref[i, :H] = s
        out_ref[i, H:] = more


def gathered(z_ref, tiles):
    parts = [
        jnp.concatenate([z_ref[2 * t, :H], z_ref[2 * t + 1, :H]], axis=0) for t in range(tiles)
    ]
    return jnp.concatenate(parts, axis=1)


def both_cores(core, mine, other):
    return jnp.where(core == 0, jnp.concatenate([mine, other], axis=1), jnp.concatenate([other, mine], axis=1))


def back_body(c_ref, z_ref, g_ref, h_ref, out_ref, rows_ref):
    tiles = g_ref.shape[1] // LANES
    factor(unfold(z_ref[2 * tiles]), rows_ref)
    z = nn(inverse_of(rows_ref), gathered(z_ref, tiles))
    y = both_cores(c_ref[0], nt(z, g_ref[...]), nt(z, h_ref[...]))
    gram = fold(nt(z, z))
    for i in range(out_ref.shape[0]):
        out_ref[i, :R] = y
        out_ref[i, R:] = gram


def last_body(c_ref, z_ref, yt_ref, a_ref, b_ref, o_ref, p_ref, out_ref, inv_ref, left_ref, rows_ref):
    core = c_ref[0]
    tiles = a_ref.shape[1] // LANES
    factor(unfold(z_ref[2 * tiles, :H]), rows_ref)
    inv = inverse_of(rows_ref)
    inv_ref[...] = inv
    left = nn(inv, yt_ref[...])
    left_ref[...] = jnp.where(core == 0, left[:, :R], left[:, R:]).T
    z = nn(inv, gathered(z_ref, tiles))
    right = [nt(z, a_ref[...]), nt(z, b_ref[...])]
    far = z_ref.shape[0] // (o_ref.shape[1] // LANES)
    near = z_ref.shape[0] // far
    feats = jnp.concatenate(
        [
            jnp.concatenate([z_ref[e * near + q, H:] for e in range(far)], axis=0)
            for q in range(near)
        ],
        axis=1,
    )
    lefts = nn(inv, feats)
    both = [nt(lefts, o_ref[...]), nt(lefts, p_ref[...])]
    gram = fold(nt(z, z))
    n = out_ref.shape[0] // 2
    mine = jnp.concatenate([both[0], right[0]], axis=1)
    other = jnp.concatenate([both[1], right[1]], axis=1)
    for c in range(2):
        tokens = jnp.where(core == c, mine, other)
        for i in range(n):
            out_ref[c * n + i, :R] = tokens
            out_ref[c * n + i, R:] = gram


def finish_body(c_ref, got_ref, inv_ref, z_ref, w_ref, right_ref, scores_ref, rows_ref):
    s = got_ref[0]
    for i in range(1, got_ref.shape[0]):
        s = s + got_ref[i]
    factor(unfold(s[R:]), rows_ref)
    inv = inverse_of(rows_ref)
    mixed = nn(lower_t_of(rows_ref), s[:R, :R])
    token_right = nn(inv, s[:R, R:])
    scores_ref[...] = jnp.sum(mixed * token_right, axis=0, keepdims=True)
    whole = nn(inv, inv_ref[...])
    core = c_ref[0]
    n = right_ref.shape[0]
    tiles = -(-n // (2 * LANES))
    mine, other = gathered(z_ref, tiles), gathered(w_ref, tiles)
    for c in range(2):
        r = nn(whole, jnp.where(core == c, mine, other))
        for t in range(tiles):
            start = (c * tiles + t) * LANES
            length = min(LANES, n - start)
            right_ref[start : start + length] = r[:, t * LANES : (t + 1) * LANES].T[:length]


def exchanged(a, axes):
    return lax.all_to_all(a, axes, split_axis=0, concat_axis=0, tiled=True)


def per_device(gradient, start_block, activations, out_grads):
    far, near = lax.axis_size("y"), lax.axis_size("z")
    cols = lax.axis_size("x")
    slots, peers = far * near, 2 * cols
    core_at = lax.axis_index("c")
    core = core_at.astype(jnp.int32).reshape(1)
    n = gradient.shape[1]
    width = -(-n // (2 * LANES)) * LANES
    piece = R // peers

    first = call(first_body, shape(peers, H, LANES), 2)(gradient, start_block)
    got = exchanged(first, PEERS)
    g, h = swapped(core, gradient, width)
    a, b = swapped(core, activations, width)
    o, p = swapped(core, out_grads, out_grads.shape[1] // 2)
    square = pltpu.VMEM((R, LANES), F32)

    parts = call(spread_first_body, shape(slots, H, LANES), 4, scalars=1)(core, got, g, h)
    for step in range(ITERS):
        arrived = exchanged(parts, CHIPS)
        if step < ITERS - 1:
            sums = call(total_body, shape(slots, H, LANES), 1)(arrived)
            z = exchanged(sums, CHIPS)
            partial = call(
                back_body, shape(peers, R + H, LANES), 4, scalars=1, scratch=[square]
            )(core, z, g, h)
            got = exchanged(partial, PEERS)
            parts, yt = call(
                spread_body,
                (shape(slots, H, LANES), shape(R, LANES)),
                4,
                scalars=1,
                scratch=[square],
            )(core, got, g, h)
    eighth = lax.axis_index("x") * 2 + core_at
    mine = lax.dynamic_slice_in_dim(yt, eighth * piece, piece, 0)
    moves = []
    for ys in range(far):
        for cs in range(2):
            for xs in range(cols):
                source = (ys * 2 + cs) * cols + xs
                target = ((2 * xs + cs) * 2 + ys % 2) * cols + ys // 2
                moves.append((source, target))
    lines = lax.ppermute(mine, ("y", "c", "x"), moves)
    sums = call(total_with_body, shape(slots, H + piece, LANES), 2)(arrived, lines)
    z = exchanged(sums, CHIPS)
    w = lax.ppermute(z[:, :H], "c", [(0, 1), (1, 0)])
    partial, inv, left = call(
        last_body,
        (shape(peers, R + H, LANES), shape(R, R), shape(R, R)),
        7,
        scalars=1,
        scratch=[square],
    )(core, z, yt, a, b, o, p)
    got = exchanged(partial, PEERS)
    right, scores = call(
        finish_body, (shape(n, R), shape(1, R)), 5, scalars=1, scratch=[square]
    )(core, got, inv, z, w)
    return (left, right, scores.reshape(-1))


def solution(mesh):
    sizes = (8, 8, 2, mesh.shape["cols"])
    torus = Mesh(mesh.devices.reshape(sizes), ("y", "z", "c", "x"))
    placed = (P(ROWS, "x"), P("x", None), P(ROWS, "x"), P(ROWS, "x"))
    return jax.shard_map(
        per_device,
        mesh=torus,
        in_specs=placed,
        out_specs=(P(ROWS, None), P("x", None), P(ROWS)),
        check_vma=False,
    )
```

```python
import functools

import jax
import jax.numpy as jnp
from jax import lax
from jax.experimental import pallas as pl
from jax.experimental.pallas import tpu as pltpu
from jax.sharding import Mesh
from jax.sharding import PartitionSpec as P

ITERS = 2
R = 64
H = R // 2
LANES = 128
F32 = jnp.float32
ROWS = ("y", "z", "c")
CHIPS = ("y", "z")
PEERS = ("c", "x")
HIGH = lax.Precision.HIGHEST

VMEM = pl.BlockSpec(memory_space=pltpu.VMEM)
SMEM = pl.BlockSpec(memory_space=pltpu.SMEM)


def nn(a, b):
    return lax.dot_general(a, b, (((1,), (0,)), ((), ())), precision=HIGH, preferred_element_type=F32)


def nt(a, b):
    return lax.dot_general(a, b, (((1,), (1,)), ((), ())), precision=HIGH, preferred_element_type=F32)


def split(a):
    high = a.astype(jnp.bfloat16)
    return high, (a - high.astype(F32)).astype(jnp.bfloat16)


def dot(a, b, dims):
    return lax.dot_general(a, b, (dims, ((), ())), preferred_element_type=F32)


def product(a, b):
    ah, al = split(a)
    bh, bl = split(b)
    dims = ((1,), (0,))
    return dot(ah, bh, dims) + (dot(al, bh, dims) + dot(ah, bl, dims))


def against(lines, z):
    n = lines.shape[0]
    gh, gl = split(lines)
    zh, zl = split(z)
    dims = ((1,), (1,))
    one = dot(jnp.concatenate([gh, gl, zh, zl], axis=0), zh, dims)
    two = dot(jnp.concatenate([gh, zl], axis=0), zl, dims)
    y = one[:n] + (one[n : 2 * n] + two[:n])
    cross = one[2 * n + R :]
    gram = one[2 * n : 2 * n + R] + (cross + cross.T + two[n:])
    return y.T, gram


def call(body, out_shape, n_in, scalars=0, scratch=()):
    specs = [SMEM] * scalars + [VMEM] * (n_in - scalars)
    outs = jax.tree.map(lambda _: VMEM, out_shape)
    return pl.pallas_call(
        body,
        out_shape=out_shape,
        in_specs=specs,
        out_specs=outs,
        scratch_shapes=list(scratch),
        compiler_params=pltpu.CompilerParams(vmem_limit_bytes=48 * 2**20),
    )


def shape(*dims):
    return jax.ShapeDtypeStruct(dims, F32)


def rsqrt(s):
    t = lax.rsqrt(s)
    return t * (1.5 - 0.5 * s * t * t)


def fold(square):
    return jnp.concatenate([square[:H], square[H:]], axis=1)


def unfold(half):
    return jnp.concatenate([half[:, :R], half[:, R:]], axis=0)


def factor(gram, rows_ref):
    b = 8
    line = lax.broadcasted_iota(jnp.int32, (R, R), 0)
    lane = lax.broadcasted_iota(jnp.int32, (R, R), 1)
    both = jnp.concatenate([gram, (line == lane).astype(F32)], axis=1)
    groups = [both[8 * g : 8 * g + 8] for g in range(R // 8)]
    sub = lax.broadcasted_iota(jnp.int32, (8, LANES), 0)
    for k in range(0, R, b):
        g0, off = divmod(k, 8)
        rows = [jnp.broadcast_to(groups[g0][off + i : off + i + 1], (8, LANES)) for i in range(b)]
        live = range(g0 if off + b < 8 else g0 + 1, R // 8)
        cols = {
            g: [jnp.broadcast_to(groups[g][:, k + j : k + j + 1], (8, LANES)) for j in range(b)]
            for g in live
        }
        low = [[None] * b for _ in range(b)]
        inv = [None] * b
        for i in range(b):
            splat = [jnp.broadcast_to(rows[i][:, k + j : k + j + 1], (8, LANES)) for j in range(i + 1)]
            for j in range(i):
                s = splat[j]
                for q in range(j):
                    s = s - low[i][q] * low[j][q]
                low[i][j] = s * inv[j]
            d = splat[i]
            for q in range(i):
                d = d - low[i][q] * low[i][q]
            inv[i] = rsqrt(d)

        def solved(lines):
            done = []
            for i in range(b):
                s = lines[i]
                for q in range(i):
                    s = s - low[i][q] * done[q]
                done.append(s * inv[i])
            return done

        new_rows = solved(rows)
        for i in range(b):
            rows_ref[k + i : k + i + 1, :] = new_rows[i][0:1]
        for g in live:
            f = solved(cols[g])
            upd = f[0] * new_rows[0]
            for i in range(1, b):
                upd = upd + f[i] * new_rows[i]
            if g == g0:
                upd = jnp.where(sub >= off + b, upd, 0.0)
            groups[g] = groups[g] - upd


def inverse_of(rows_ref):
    line = lax.broadcasted_iota(jnp.int32, (R, R), 0)
    lane = lax.broadcasted_iota(jnp.int32, (R, R), 1)
    return jnp.where(line >= lane, rows_ref[:, R:], 0.0)


def lower_t_of(rows_ref):
    line = lax.broadcasted_iota(jnp.int32, (R, R), 0)
    lane = lax.broadcasted_iota(jnp.int32, (R, R), 1)
    return jnp.where(line <= lane, rows_ref[:, :R], 0.0)


def halves(core, a_ref, keep_ref, send_ref):
    width = keep_ref.shape[1]
    rest = a_ref.shape[1] - width

    @pl.when(core == 0)
    def _():
        keep_ref[...] = a_ref[:, :width]
        send_ref[:, :rest] = a_ref[:, width:]
        if rest < width:
            send_ref[:, rest:] = jnp.zeros((send_ref.shape[0], width - rest), F32)

    @pl.when(core != 0)
    def _():
        send_ref[...] = a_ref[:, :width]
        keep_ref[:, :rest] = a_ref[:, width:]
        if rest < width:
            keep_ref[:, rest:] = jnp.zeros((send_ref.shape[0], width - rest), F32)


def halves_body(c_ref, a_ref, keep_ref, send_ref):
    halves(c_ref[0], a_ref, keep_ref, send_ref)


def swapped(core, a, width):
    lines = a.shape[0]
    keep, send = call(halves_body, (shape(lines, width), shape(lines, width)), 2, scalars=1)(core, a)
    return keep, other_core(send)


def other_core(a):
    return lax.ppermute(a, "c", [(0, 1), (1, 0)])


def first_body(c_ref, g_ref, o_ref, out_ref, keep_ref, send_ref):
    gh, gl = split(g_ref[...])
    oh, ol = split(o_ref[...])
    dims = ((1,), (1,))
    n = g_ref.shape[0]
    one = dot(jnp.concatenate([gh, gl], axis=0), oh, dims)
    y = fold((one[:n] + (one[n:] + dot(gh, ol, dims))).T)
    for i in range(out_ref.shape[0]):
        out_ref[i] = y
    halves(c_ref[0], g_ref, keep_ref, send_ref)


def put_slots(yt, g_refs, core, out_ref):
    lines = jnp.concatenate([g_refs[0][...], g_refs[1][...]], axis=0)
    z = product(in_turn(core, yt), lines)
    tiles = z.shape[1] // LANES
    for t in range(tiles):
        part = z[:, t * LANES : (t + 1) * LANES]
        out_ref[2 * t] = part[:H]
        out_ref[2 * t + 1] = part[H:]
    out_ref[2 * tiles] = fold(nt(yt, yt))
    for s in range(2 * tiles + 1, out_ref.shape[0]):
        out_ref[s] = jnp.zeros((H, LANES), F32)


def spread_first_body(c_ref, got_ref, g_ref, h_ref, out_ref):
    n = got_ref.shape[0] // 2
    parts = []
    for c in range(2):
        s = got_ref[c * n]
        for i in range(1, n):
            s = s + got_ref[c * n + i]
        parts.append(unfold(s))
    yt = jnp.concatenate(parts, axis=1)
    put_slots(yt, (g_ref, h_ref), c_ref[0], out_ref)


def spread_body(c_ref, got_ref, g_ref, h_ref, out_ref, yt_ref, rows_ref):
    s = got_ref[0]
    for i in range(1, got_ref.shape[0]):
        s = s + got_ref[i]
    factor(unfold(s[R:]), rows_ref)
    yt = nn(inverse_of(rows_ref), s[:R])
    yt_ref[...] = yt
    put_slots(yt, (g_ref, h_ref), c_ref[0], out_ref)


def total_body(got_ref, out_ref):
    n = got_ref.shape[0]
    s = got_ref[0]
    for i in range(1, n):
        s = s + got_ref[i]
    for i in range(n):
        out_ref[i] = s


def total_with_body(got_ref, more_ref, out_ref):
    n = got_ref.shape[0]
    s = got_ref[0]
    for i in range(1, n):
        s = s + got_ref[i]
    more = more_ref[...]
    for i in range(n):
        out_ref[i, :H] = s
        out_ref[i, H:] = more


def gathered(z_ref, tiles):
    parts = [
        jnp.concatenate([z_ref[2 * t, :H], z_ref[2 * t + 1, :H]], axis=0) for t in range(tiles)
    ]
    return jnp.concatenate(parts, axis=1)


def in_turn(core, pair):
    turned = jnp.concatenate([pair[:, R:], pair[:, :R]], axis=1)
    return jnp.where(core == 0, pair, turned)


def back_body(c_ref, z_ref, g_ref, h_ref, out_ref, rows_ref):
    tiles = g_ref.shape[1] // LANES
    factor(unfold(z_ref[2 * tiles]), rows_ref)
    z = product(inverse_of(rows_ref), gathered(z_ref, tiles))
    y, gram = against(jnp.concatenate([g_ref[...], h_ref[...]], axis=0), z)
    y = in_turn(c_ref[0], y)
    gram = fold(gram)
    for i in range(out_ref.shape[0]):
        out_ref[i, :R] = y
        out_ref[i, R:] = gram


def last_body(c_ref, z_ref, yt_ref, a_ref, b_ref, o_ref, p_ref, out_ref, inv_ref, left_ref, rows_ref):
    core = c_ref[0]
    tiles = a_ref.shape[1] // LANES
    factor(unfold(z_ref[2 * tiles, :H]), rows_ref)
    inv = inverse_of(rows_ref)
    inv_ref[...] = inv
    left = nn(inv, yt_ref[...])
    left_ref[...] = jnp.where(core == 0, left[:, :R], left[:, R:]).T
    z = product(inv, gathered(z_ref, tiles))
    rights, gram = against(jnp.concatenate([a_ref[...], b_ref[...]], axis=0), z)
    near = o_ref.shape[1] // LANES
    far = z_ref.shape[0] // near
    feats = jnp.concatenate(
        [
            jnp.concatenate([z_ref[e * near + q, H:] for e in range(far)], axis=0)
            for q in range(near)
        ],
        axis=1,
    )
    lefts, _ = against(jnp.concatenate([o_ref[...], p_ref[...]], axis=0), nn(inv, feats))
    gram = fold(gram)
    n = out_ref.shape[0] // 2
    mine = jnp.concatenate([lefts[:, :R], rights[:, :R]], axis=1)
    other = jnp.concatenate([lefts[:, R:], rights[:, R:]], axis=1)
    for c in range(2):
        tokens = jnp.where(core == c, mine, other)
        for i in range(n):
            out_ref[c * n + i, :R] = tokens
            out_ref[c * n + i, R:] = gram


def finish_body(c_ref, got_ref, inv_ref, z_ref, w_ref, right_ref, scores_ref, rows_ref):
    s = got_ref[0]
    for i in range(1, got_ref.shape[0]):
        s = s + got_ref[i]
    factor(unfold(s[R:]), rows_ref)
    inv = inverse_of(rows_ref)
    mixed = nn(lower_t_of(rows_ref), s[:R, :R])
    token_right = nn(inv, s[:R, R:])
    scores_ref[...] = jnp.sum(mixed * token_right, axis=0, keepdims=True)
    whole = nn(inv, inv_ref[...])
    core = c_ref[0]
    n = right_ref.shape[1]
    tiles = -(-n // (2 * LANES))
    width = tiles * LANES
    mine, other = gathered(z_ref, tiles), gathered(w_ref, tiles)
    right_ref[:, :width] = product(whole, jnp.where(core == 0, mine, other))
    right_ref[:, width:] = product(whole, jnp.where(core == 0, other, mine))[:, : n - width]


def exchanged(a, axes):
    return lax.all_to_all(a, axes, split_axis=0, concat_axis=0, tiled=True)


def per_device(gradient, start_block, activations, out_grads):
    far, near = lax.axis_size("y"), lax.axis_size("z")
    cols = lax.axis_size("x")
    slots, peers = far * near, 2 * cols
    core_at = lax.axis_index("c")
    core = core_at.astype(jnp.int32).reshape(1)
    n = gradient.shape[1]
    width = -(-n // (2 * LANES)) * LANES
    piece = R // peers

    lines = gradient.shape[0]
    first, g, send = call(
        first_body, (shape(peers, H, LANES), shape(lines, width), shape(lines, width)), 3, scalars=1
    )(core, gradient, start_block.T)
    h = other_core(send)
    got = exchanged(first, PEERS)
    a, b = swapped(core, activations, width)
    o, p = swapped(core, out_grads, out_grads.shape[1] // 2)
    square = pltpu.VMEM((R, LANES), F32)

    parts = call(spread_first_body, shape(slots, H, LANES), 4, scalars=1)(core, got, g, h)
    for step in range(ITERS):
        arrived = exchanged(parts, CHIPS)
        if step < ITERS - 1:
            arrived, a, b, o, p = lax.optimization_barrier((arrived, a, b, o, p))
            sums = call(total_body, shape(slots, H, LANES), 1)(arrived)
            z = exchanged(sums, CHIPS)
            partial = call(
                back_body, shape(peers, R + H, LANES), 4, scalars=1, scratch=[square]
            )(core, z, g, h)
            got = exchanged(partial, PEERS)
            parts, yt = call(
                spread_body,
                (shape(slots, H, LANES), shape(R, LANES)),
                4,
                scalars=1,
                scratch=[square],
            )(core, got, g, h)
    eighth = lax.axis_index("x") * 2 + core_at
    mine = lax.dynamic_slice_in_dim(yt, eighth * piece, piece, 0)
    moves = []
    for ys in range(far):
        for cs in range(2):
            for xs in range(cols):
                source = (ys * 2 + cs) * cols + xs
                target = ((2 * xs + cs) * 2 + ys % 2) * cols + ys // 2
                moves.append((source, target))
    lines = lax.ppermute(mine, ("y", "c", "x"), moves)
    sums = call(total_with_body, shape(slots, H + piece, LANES), 2)(arrived, lines)
    z = exchanged(sums, CHIPS)
    w = other_core(z[:, :H])
    partial, inv, left = call(
        last_body,
        (shape(peers, R + H, LANES), shape(R, R), shape(R, R)),
        7,
        scalars=1,
        scratch=[square],
    )(core, z, yt, a, b, o, p)
    got = exchanged(partial, PEERS)
    right, scores = call(
        finish_body, (shape(R, n), shape(1, R)), 5, scalars=1, scratch=[square]
    )(core, got, inv, z, w)
    return (left, right.T, scores.reshape(-1))


def solution(mesh):
    sizes = (8, 8, 2, mesh.shape["cols"])
    torus = Mesh(mesh.devices.reshape(sizes), ("y", "z", "c", "x"))
    placed = (P(ROWS, "x"), P("x", None), P(ROWS, "x"), P(ROWS, "x"))
    return jax.shard_map(
        per_device,
        mesh=torus,
        in_specs=placed,
        out_specs=(P(ROWS, None), P("x", None), P(ROWS)),
        check_vma=False,
    )
```

```python
import jax
import jax.numpy as jnp
from jax import lax
from jax.experimental import pallas as pl
from jax.experimental.pallas import tpu as pltpu
from jax.sharding import Mesh
from jax.sharding import PartitionSpec as P

R = 64
H = R // 2
LANES = 128
F32 = jnp.float32
ROWS = ("y", "z", "c")
CHIPS = ("y", "z")
PEERS = ("c", "x")
HIGH = lax.Precision.HIGHEST

VMEM = pl.BlockSpec(memory_space=pltpu.VMEM)
SMEM = pl.BlockSpec(memory_space=pltpu.SMEM)


def nn(a, b):
    return lax.dot_general(a, b, (((1,), (0,)), ((), ())), precision=HIGH, preferred_element_type=F32)


def nt(a, b):
    return lax.dot_general(a, b, (((1,), (1,)), ((), ())), precision=HIGH, preferred_element_type=F32)


def split(a):
    high = a.astype(jnp.bfloat16)
    rest = a - high.astype(F32)
    middle = rest.astype(jnp.bfloat16)
    return high, middle, (rest - middle.astype(F32)).astype(jnp.bfloat16)


def dot(a, b, dims):
    return lax.dot_general(a, b, (dims, ((), ())), preferred_element_type=F32)


def product(a, b):
    n = a.shape[0]
    lines = jnp.concatenate(split(a), axis=0)
    high, middle, low = split(b)
    dims = ((1,), (0,))
    one = dot(lines, high, dims)
    two = dot(lines[: 2 * n], middle, dims)
    three = dot(lines[:n], low, dims)
    return one[:n] + (one[n : 2 * n] + two[:n] + (one[2 * n :] + two[n:] + three))


def against(lines, z):
    parts = split(z)
    blocks = [*split(lines), *parts]
    n = lines.shape[0]
    out = dot(jnp.concatenate(blocks, axis=0), jnp.concatenate(parts, axis=0), ((1,), (1,)))

    def total(start, length):
        def block(i, j):
            top = start + i * length
            return out[top : top + length, j * R : (j + 1) * R]

        small = block(1, 1) + block(0, 2) + block(2, 0)
        return block(0, 0) + (block(0, 1) + block(1, 0) + small)

    return total(0, n).T, total(3 * n, R)


def call(body, out_shape, n_in, scalars=0, scratch=()):
    specs = [SMEM] * scalars + [VMEM] * (n_in - scalars)
    outs = jax.tree.map(lambda _: VMEM, out_shape)
    return pl.pallas_call(
        body,
        out_shape=out_shape,
        in_specs=specs,
        out_specs=outs,
        scratch_shapes=list(scratch),
        compiler_params=pltpu.CompilerParams(vmem_limit_bytes=48 * 2**20),
    )


def shape(*dims):
    return jax.ShapeDtypeStruct(dims, F32)


def rsqrt(s):
    t = lax.rsqrt(s)
    return t * (1.5 - 0.5 * s * t * t)


def fold(square):
    return jnp.concatenate([square[:H], square[H:]], axis=1)


def unfold(half):
    return jnp.concatenate([half[:, :R], half[:, R:]], axis=0)


def factor(gram, rows_ref):
    b = 8
    line = lax.broadcasted_iota(jnp.int32, (R, R), 0)
    lane = lax.broadcasted_iota(jnp.int32, (R, R), 1)
    both = jnp.concatenate([gram, (line == lane).astype(F32)], axis=1)
    groups = [both[8 * g : 8 * g + 8] for g in range(R // 8)]
    sub = lax.broadcasted_iota(jnp.int32, (8, LANES), 0)
    for k in range(0, R, b):
        g0, off = divmod(k, 8)
        rows = [jnp.broadcast_to(groups[g0][off + i : off + i + 1], (8, LANES)) for i in range(b)]
        live = range(g0 if off + b < 8 else g0 + 1, R // 8)
        cols = {
            g: [jnp.broadcast_to(groups[g][:, k + j : k + j + 1], (8, LANES)) for j in range(b)]
            for g in live
        }
        low = [[None] * b for _ in range(b)]
        inv = [None] * b
        for i in range(b):
            splat = [jnp.broadcast_to(rows[i][:, k + j : k + j + 1], (8, LANES)) for j in range(i + 1)]
            for j in range(i):
                s = splat[j]
                for q in range(j):
                    s = s - low[i][q] * low[j][q]
                low[i][j] = s * inv[j]
            d = splat[i]
            for q in range(i):
                d = d - low[i][q] * low[i][q]
            inv[i] = rsqrt(d)

        def solved(lines):
            done = []
            for i in range(b):
                s = lines[i]
                for q in range(i):
                    s = s - low[i][q] * done[q]
                done.append(s * inv[i])
            return done

        new_rows = solved(rows)
        for i in range(b):
            rows_ref[k + i : k + i + 1, :] = new_rows[i][0:1]
        for g in live:
            f = solved(cols[g])
            upd = f[0] * new_rows[0]
            for i in range(1, b):
                upd = upd + f[i] * new_rows[i]
            if g == g0:
                upd = jnp.where(sub >= off + b, upd, 0.0)
            groups[g] = groups[g] - upd


def inverse_of(rows_ref):
    line = lax.broadcasted_iota(jnp.int32, (R, R), 0)
    lane = lax.broadcasted_iota(jnp.int32, (R, R), 1)
    return jnp.where(line >= lane, rows_ref[:, R:], 0.0)


def lower_t_of(rows_ref):
    line = lax.broadcasted_iota(jnp.int32, (R, R), 0)
    lane = lax.broadcasted_iota(jnp.int32, (R, R), 1)
    return jnp.where(line <= lane, rows_ref[:, :R], 0.0)


def halves(core, a_ref, keep_ref, send_ref):
    width = keep_ref.shape[1]
    rest = a_ref.shape[1] - width

    @pl.when(core == 0)
    def _():
        keep_ref[...] = a_ref[:, :width]
        send_ref[:, :rest] = a_ref[:, width:]
        if rest < width:
            send_ref[:, rest:] = jnp.zeros((send_ref.shape[0], width - rest), F32)

    @pl.when(core != 0)
    def _():
        send_ref[...] = a_ref[:, :width]
        keep_ref[:, :rest] = a_ref[:, width:]
        if rest < width:
            keep_ref[:, rest:] = jnp.zeros((send_ref.shape[0], width - rest), F32)


def halves_body(c_ref, a_ref, keep_ref, send_ref):
    halves(c_ref[0], a_ref, keep_ref, send_ref)


def swapped(core, a, width):
    lines = a.shape[0]
    keep, send = call(halves_body, (shape(lines, width), shape(lines, width)), 2, scalars=1)(core, a)
    return keep, other_core(send)


def other_core(a):
    return lax.ppermute(a, "c", [(0, 1), (1, 0)])


def first_body(c_ref, g_ref, o_ref, out_ref, keep_ref, send_ref):
    y = fold(against(g_ref[...], o_ref[...])[0])
    for i in range(out_ref.shape[0]):
        out_ref[i] = y
    halves(c_ref[0], g_ref, keep_ref, send_ref)


def put_slots(yt, g_refs, core, out_ref):
    lines = jnp.concatenate([g_refs[0][...], g_refs[1][...]], axis=0)
    z = product(in_turn(core, yt), lines)
    tiles = z.shape[1] // LANES
    for t in range(tiles):
        part = z[:, t * LANES : (t + 1) * LANES]
        out_ref[2 * t] = part[:H]
        out_ref[2 * t + 1] = part[H:]
    for s in range(2 * tiles, out_ref.shape[0]):
        out_ref[s] = jnp.zeros((H, LANES), F32)


def spread_first_body(c_ref, got_ref, g_ref, h_ref, out_ref, gram_ref):
    n = got_ref.shape[0] // 2
    parts = []
    for c in range(2):
        s = got_ref[c * n]
        for i in range(1, n):
            s = s + got_ref[c * n + i]
        parts.append(unfold(s))
    yt = jnp.concatenate(parts, axis=1)
    put_slots(yt, (g_ref, h_ref), c_ref[0], out_ref)
    gram_ref[...] = fold(nt(yt, yt))


def spread_body(c_ref, got_ref, g_ref, h_ref, out_ref, raw_ref):
    s = got_ref[0]
    for i in range(1, got_ref.shape[0]):
        s = s + got_ref[i]
    raw_ref[...] = s
    put_slots(s[:R], (g_ref, h_ref), c_ref[0], out_ref)


def factor_body(gram_ref, inv_ref, rows_ref):
    factor(unfold(gram_ref[...]), rows_ref)
    inv_ref[...] = inverse_of(rows_ref)


def normal_body(raw_ref, inv_ref, gram_ref, rows_ref):
    factor(unfold(raw_ref[R:]), rows_ref)
    inv = inverse_of(rows_ref)
    inv_ref[...] = inv
    yt = nn(inv, raw_ref[:R])
    gram_ref[...] = fold(nt(yt, yt))


def left_body(c_ref, gram_ref, raw_ref, prior_ref, inv_ref, left_ref, rows_ref):
    factor(unfold(gram_ref[...]), rows_ref)
    inv = inverse_of(rows_ref)
    left = nn(inv, nn(prior_ref[...], raw_ref[:R]))
    left_ref[...] = jnp.where(c_ref[0] == 0, left[:, :R], left[:, R:]).T
    inv_ref[...] = nn(inv, prior_ref[...])


def total_body(got_ref, out_ref):
    n = got_ref.shape[0]
    s = got_ref[0]
    for i in range(1, n):
        s = s + got_ref[i]
    for i in range(n):
        out_ref[i] = s


def total_with_body(got_ref, more_ref, out_ref):
    n = got_ref.shape[0]
    s = got_ref[0]
    for i in range(1, n):
        s = s + got_ref[i]
    more = more_ref[...]
    for i in range(n):
        out_ref[i, :H] = s
        out_ref[i, H:] = more


def gathered(z_ref, tiles):
    parts = [
        jnp.concatenate([z_ref[2 * t, :H], z_ref[2 * t + 1, :H]], axis=0) for t in range(tiles)
    ]
    return jnp.concatenate(parts, axis=1)


def in_turn(core, pair):
    turned = jnp.concatenate([pair[:, R:], pair[:, :R]], axis=1)
    return jnp.where(core == 0, pair, turned)


def back_body(c_ref, z_ref, g_ref, h_ref, inv_ref, out_ref):
    tiles = g_ref.shape[1] // LANES
    z = product(inv_ref[...], gathered(z_ref, tiles))
    y, gram = against(jnp.concatenate([g_ref[...], h_ref[...]], axis=0), z)
    y = in_turn(c_ref[0], y)
    gram = fold(gram)
    for i in range(out_ref.shape[0]):
        out_ref[i, :R] = y
        out_ref[i, R:] = gram


def last_body(c_ref, z_ref, inv_ref, a_ref, b_ref, o_ref, p_ref, out_ref):
    core = c_ref[0]
    tiles = a_ref.shape[1] // LANES
    inv = inv_ref[...]
    z = product(inv, gathered(z_ref, tiles))
    rights, gram = against(jnp.concatenate([a_ref[...], b_ref[...]], axis=0), z)
    near = o_ref.shape[1] // LANES
    far = z_ref.shape[0] // near
    feats = jnp.concatenate(
        [
            jnp.concatenate([z_ref[e * near + q, H:] for e in range(far)], axis=0)
            for q in range(near)
        ],
        axis=1,
    )
    lefts, _ = against(jnp.concatenate([o_ref[...], p_ref[...]], axis=0), nn(inv, feats))
    gram = fold(gram)
    n = out_ref.shape[0] // 2
    mine = jnp.concatenate([lefts[:, :R], rights[:, :R]], axis=1)
    other = jnp.concatenate([lefts[:, R:], rights[:, R:]], axis=1)
    for c in range(2):
        tokens = jnp.where(core == c, mine, other)
        for i in range(n):
            out_ref[c * n + i, :R] = tokens
            out_ref[c * n + i, R:] = gram


def finish_body(c_ref, got_ref, inv_ref, z_ref, w_ref, right_ref, scores_ref, rows_ref):
    s = got_ref[0]
    for i in range(1, got_ref.shape[0]):
        s = s + got_ref[i]
    factor(unfold(s[R:]), rows_ref)
    inv = inverse_of(rows_ref)
    mixed = nn(lower_t_of(rows_ref), s[:R, :R])
    token_right = nn(inv, s[:R, R:])
    scores_ref[...] = jnp.sum(mixed * token_right, axis=0, keepdims=True)
    whole = nn(inv, inv_ref[...])
    core = c_ref[0]
    n = right_ref.shape[1]
    tiles = -(-n // (2 * LANES))
    width = tiles * LANES
    mine, other = gathered(z_ref, tiles), gathered(w_ref, tiles)
    right_ref[:, :width] = product(whole, jnp.where(core == 0, mine, other))
    right_ref[:, width:] = product(whole, jnp.where(core == 0, other, mine))[:, : n - width]


def exchanged(a, axes):
    return lax.all_to_all(a, axes, split_axis=0, concat_axis=0, tiled=True)


def summed(part, rounds):
    for axis, bit in rounds:
        pairs = [(i, i ^ bit) for i in range(lax.axis_size(axis))]
        part = part + lax.ppermute(part, axis, pairs)
    return part


def per_device(gradient, start_block, activations, out_grads):
    far, near = lax.axis_size("y"), lax.axis_size("z")
    cols = lax.axis_size("x")
    slots, peers = far * near, 2 * cols
    core_at = lax.axis_index("c")
    core = core_at.astype(jnp.int32).reshape(1)
    n = gradient.shape[1]
    width = -(-n // (2 * LANES)) * LANES
    piece = R // peers

    rounds = [(axis, 1 << k) for axis in CHIPS for k in range(lax.axis_size(axis).bit_length() - 1)]
    early, late = rounds[: len(rounds) // 2], rounds[len(rounds) // 2 :]
    lines = gradient.shape[0]
    first, g, send = call(
        first_body, (shape(peers, H, LANES), shape(lines, width), shape(lines, width)), 3, scalars=1
    )(core, gradient, start_block.T)
    h = other_core(send)
    got = exchanged(first, PEERS)
    a, b = swapped(core, activations, width)
    o, p = swapped(core, out_grads, out_grads.shape[1] // 2)
    square = [pltpu.VMEM((R, LANES), F32)]
    block, whole = shape(slots, H, LANES), shape(peers, R + H, LANES)
    half, small = shape(H, LANES), shape(R, R)

    parts, gram = call(spread_first_body, (block, half), 4, scalars=1)(core, got, g, h)
    arrived = exchanged(parts, CHIPS)
    gram = summed(gram, early)
    arrived, gram, a, b, o, p = lax.optimization_barrier((arrived, gram, a, b, o, p))
    z = exchanged(call(total_body, block, 1)(arrived), CHIPS)
    inv = call(factor_body, small, 1, scratch=square)(summed(gram, late))
    partial = call(back_body, whole, 5, scalars=1)(core, z, g, h, inv)

    got = exchanged(partial, PEERS)
    raw_shape = shape(R + H, LANES)
    parts, raw = call(spread_body, (block, raw_shape), 4, scalars=1)(core, got, g, h)
    arrived = exchanged(parts, CHIPS)
    prior, gram = call(normal_body, (small, half), 1, scratch=square)(raw)
    gram = summed(gram, early)
    eighth = lax.axis_index("x") * 2 + core_at
    mine = lax.dynamic_slice_in_dim(raw, eighth * piece, piece, 0)
    moves = []
    for ys in range(far):
        for cs in range(2):
            for xs in range(cols):
                source = (ys * 2 + cs) * cols + xs
                target = ((2 * xs + cs) * 2 + ys % 2) * cols + ys // 2
                moves.append((source, target))
    lines = lax.ppermute(mine, ("y", "c", "x"), moves)
    arrived, gram, lines = lax.optimization_barrier((arrived, gram, lines))
    z = exchanged(
        call(total_with_body, shape(slots, H + piece, LANES), 2)(arrived, lines), CHIPS
    )
    inv, left = call(left_body, (small, small), 4, scalars=1, scratch=square)(
        core, summed(gram, late), raw, prior
    )
    z, inv, left = lax.optimization_barrier((z, inv, left))
    w = other_core(z[:, :H])
    partial = call(last_body, whole, 7, scalars=1)(core, z, inv, a, b, o, p)
    got = exchanged(partial, PEERS)
    right, scores = call(
        finish_body, (shape(R, n), shape(1, R)), 5, scalars=1, scratch=square
    )(core, got, inv, z, w)
    return (left, right.T, scores.reshape(-1))


def solution(mesh):
    sizes = (8, 8, 2, mesh.shape["cols"])
    torus = Mesh(mesh.devices.reshape(sizes), ("y", "z", "c", "x"))
    placed = (P(ROWS, "x"), P("x", None), P(ROWS, "x"), P(ROWS, "x"))
    return jax.shard_map(
        per_device,
        mesh=torus,
        in_specs=placed,
        out_specs=(P(ROWS, None), P("x", None), P(ROWS)),
        check_vma=False,
    )
```

```python
import functools

import jax
import jax.numpy as jnp
from jax import lax
from jax.experimental import pallas as pl
from jax.experimental.pallas import tpu as pltpu
from jax.sharding import Mesh
from jax.sharding import PartitionSpec as P

R = 64
H = R // 2
LANES = 128
F32 = jnp.float32
ROWS = ("y", "z", "c")
CHIPS = ("y", "z")
PEERS = ("c", "x")
HIGH = lax.Precision.HIGHEST

VMEM = pl.BlockSpec(memory_space=pltpu.VMEM)
SMEM = pl.BlockSpec(memory_space=pltpu.SMEM)


def nn(a, b):
    return lax.dot_general(a, b, (((1,), (0,)), ((), ())), precision=HIGH, preferred_element_type=F32)


def nt(a, b):
    return lax.dot_general(a, b, (((1,), (1,)), ((), ())), precision=HIGH, preferred_element_type=F32)


def split(a):
    high = a.astype(jnp.bfloat16)
    rest = a - high.astype(F32)
    middle = rest.astype(jnp.bfloat16)
    return high, middle, (rest - middle.astype(F32)).astype(jnp.bfloat16)


def dot(a, b, dims):
    return lax.dot_general(a, b, (dims, ((), ())), preferred_element_type=F32)


def product(a, b):
    n = a.shape[0]
    lines = jnp.concatenate(split(a), axis=0)
    high, middle, low = split(b)
    dims = ((1,), (0,))
    one = dot(lines, high, dims)
    two = dot(lines[: 2 * n], middle, dims)
    three = dot(lines[:n], low, dims)
    return one[:n] + (one[n : 2 * n] + two[:n] + (one[2 * n :] + two[n:] + three))


def against(lines, z):
    parts = split(z)
    blocks = [*split(lines), *parts]
    n = lines.shape[0]
    out = dot(jnp.concatenate(blocks, axis=0), jnp.concatenate(parts, axis=0), ((1,), (1,)))

    def total(start, length):
        def block(i, j):
            top = start + i * length
            return out[top : top + length, j * R : (j + 1) * R]

        small = block(1, 1) + block(0, 2) + block(2, 0)
        return block(0, 0) + (block(0, 1) + block(1, 0) + small)

    return total(0, n).T, total(3 * n, R)


def call(body, out_shape, n_in, scalars=0, scratch=()):
    specs = [SMEM] * scalars + [VMEM] * (n_in - scalars)
    outs = jax.tree.map(lambda _: VMEM, out_shape)
    return pl.pallas_call(
        body,
        out_shape=out_shape,
        in_specs=specs,
        out_specs=outs,
        scratch_shapes=list(scratch),
        compiler_params=pltpu.CompilerParams(vmem_limit_bytes=48 * 2**20),
    )


def shape(*dims):
    return jax.ShapeDtypeStruct(dims, F32)


def rsqrt(s):
    t = lax.rsqrt(s)
    return t * (1.5 - 0.5 * s * t * t)


def fold(square):
    return jnp.concatenate([square[:H], square[H:]], axis=1)


def unfold(half):
    return jnp.concatenate([half[:, :R], half[:, R:]], axis=0)


def factor(gram, rows_ref):
    b = 8
    line = lax.broadcasted_iota(jnp.int32, (R, R), 0)
    lane = lax.broadcasted_iota(jnp.int32, (R, R), 1)
    both = jnp.concatenate([gram, (line == lane).astype(F32)], axis=1)
    groups = [both[8 * g : 8 * g + 8] for g in range(R // 8)]
    sub = lax.broadcasted_iota(jnp.int32, (8, LANES), 0)
    for k in range(0, R, b):
        g0, off = divmod(k, 8)
        rows = [jnp.broadcast_to(groups[g0][off + i : off + i + 1], (8, LANES)) for i in range(b)]
        live = range(g0 if off + b < 8 else g0 + 1, R // 8)
        cols = {
            g: [jnp.broadcast_to(groups[g][:, k + j : k + j + 1], (8, LANES)) for j in range(b)]
            for g in live
        }
        low = [[None] * b for _ in range(b)]
        inv = [None] * b
        for i in range(b):
            splat = [jnp.broadcast_to(rows[i][:, k + j : k + j + 1], (8, LANES)) for j in range(i + 1)]
            for j in range(i):
                s = splat[j]
                for q in range(j):
                    s = s - low[i][q] * low[j][q]
                low[i][j] = s * inv[j]
            d = splat[i]
            for q in range(i):
                d = d - low[i][q] * low[i][q]
            inv[i] = rsqrt(d)

        def solved(lines):
            done = []
            for i in range(b):
                s = lines[i]
                for q in range(i):
                    s = s - low[i][q] * done[q]
                done.append(s * inv[i])
            return done

        new_rows = solved(rows)
        for i in range(b):
            rows_ref[k + i : k + i + 1, :] = new_rows[i][0:1]
        for g in live:
            f = solved(cols[g])
            upd = f[0] * new_rows[0]
            for i in range(1, b):
                upd = upd + f[i] * new_rows[i]
            if g == g0:
                upd = jnp.where(sub >= off + b, upd, 0.0)
            groups[g] = groups[g] - upd


def inverse_of(rows_ref):
    line = lax.broadcasted_iota(jnp.int32, (R, R), 0)
    lane = lax.broadcasted_iota(jnp.int32, (R, R), 1)
    return jnp.where(line >= lane, rows_ref[:, R:], 0.0)


def lower_t_of(rows_ref):
    line = lax.broadcasted_iota(jnp.int32, (R, R), 0)
    lane = lax.broadcasted_iota(jnp.int32, (R, R), 1)
    return jnp.where(line <= lane, rows_ref[:, :R], 0.0)


def halves(core, a_ref, keep_ref, send_ref):
    width = keep_ref.shape[1]
    rest = a_ref.shape[1] - width

    @pl.when(core == 0)
    def _():
        keep_ref[...] = a_ref[:, :width]
        send_ref[:, :rest] = a_ref[:, width:]
        if rest < width:
            send_ref[:, rest:] = jnp.zeros((send_ref.shape[0], width - rest), F32)

    @pl.when(core != 0)
    def _():
        send_ref[...] = a_ref[:, :width]
        keep_ref[:, :rest] = a_ref[:, width:]
        if rest < width:
            keep_ref[:, rest:] = jnp.zeros((send_ref.shape[0], width - rest), F32)


def halves_body(c_ref, a_ref, keep_ref, send_ref):
    halves(c_ref[0], a_ref, keep_ref, send_ref)


def swapped(core, a, width):
    lines = a.shape[0]
    keep, send = call(halves_body, (shape(lines, width), shape(lines, width)), 2, scalars=1)(core, a)
    return keep, other_core(send)


def other_core(a):
    return lax.ppermute(a, "c", [(0, 1), (1, 0)])


def first_body(c_ref, g_ref, o_ref, out_ref, keep_ref, send_ref):
    y = fold(against(g_ref[...], o_ref[...])[0])
    for i in range(out_ref.shape[0]):
        out_ref[i] = y
    halves(c_ref[0], g_ref, keep_ref, send_ref)


def put_lines(yt, gram, g_refs, core, out_ref):
    lines = jnp.concatenate([g_refs[0][...], g_refs[1][...]], axis=0)
    z = product(in_turn(core, yt), lines)
    tiles = z.shape[1] // LANES
    for t in range(tiles):
        out_ref[t * R : (t + 1) * R] = z[:, t * LANES : (t + 1) * LANES]
    out_ref[tiles * R : tiles * R + H] = fold(gram)
    rest = out_ref.shape[0] - tiles * R - H
    if rest:
        out_ref[tiles * R + H :] = jnp.zeros((rest, LANES), F32)


def spread_first_body(c_ref, got_ref, g_ref, h_ref, out_ref):
    n = got_ref.shape[0] // 2
    parts = []
    for c in range(2):
        s = got_ref[c * n]
        for i in range(1, n):
            s = s + got_ref[c * n + i]
        parts.append(unfold(s))
    yt = jnp.concatenate(parts, axis=1)
    put_lines(yt, nt(yt, yt), (g_ref, h_ref), c_ref[0], out_ref)


def spread_body(c_ref, got_ref, g_ref, h_ref, out_ref, yt_ref, rows_ref):
    s = total_of(got_ref)
    factor(unfold(s[R:]), rows_ref)
    yt = nn(inverse_of(rows_ref), s[:R])
    yt_ref[...] = yt
    put_lines(yt, nt(yt, yt), (g_ref, h_ref), c_ref[0], out_ref)


def total_of(got_ref):
    s = got_ref[0]
    for i in range(1, got_ref.shape[0]):
        s = s + got_ref[i]
    return s


def cut_body(got_ref, out_ref):
    s = total_of(got_ref)
    n = out_ref.shape[1]
    for i in range(out_ref.shape[0]):
        out_ref[i] = s[i * n : (i + 1) * n]


def total_body(got_ref, out_ref):
    s = total_of(got_ref)
    for i in range(out_ref.shape[0]):
        out_ref[i] = s


def total_with_body(got_ref, more_ref, out_ref):
    s = total_of(got_ref)
    n = s.shape[0]
    more = more_ref[...]
    for i in range(out_ref.shape[0]):
        out_ref[i, :n] = s
        out_ref[i, n:] = more


def joined_body(lines, got_ref, out_ref):
    n = got_ref.shape[0]
    heads = [got_ref[i, :lines] for i in range(n)]
    tails = [got_ref[i, lines:] for i in range(n) if got_ref.shape[1] > lines]
    s = jnp.concatenate(heads + tails, axis=0)
    for i in range(out_ref.shape[0]):
        out_ref[i] = s


def lines_of(z_ref, start, length, per):
    parts = []
    while length:
        i, at = divmod(start, per)
        n = min(length, per - at)
        parts.append(z_ref[i, at : at + n])
        start, length = start + n, length - n
    return jnp.concatenate(parts, axis=0) if len(parts) > 1 else parts[0]


def gathered(z_ref, tiles, per):
    return jnp.concatenate([lines_of(z_ref, t * R, R, per) for t in range(tiles)], axis=1)


def in_turn(core, pair):
    turned = jnp.concatenate([pair[:, R:], pair[:, :R]], axis=1)
    return jnp.where(core == 0, pair, turned)


def back_body(c_ref, z_ref, g_ref, h_ref, out_ref, rows_ref):
    tiles = g_ref.shape[1] // LANES
    per = z_ref.shape[1]
    factor(unfold(lines_of(z_ref, tiles * R, H, per)), rows_ref)
    z = product(inverse_of(rows_ref), gathered(z_ref, tiles, per))
    y, gram = against(jnp.concatenate([g_ref[...], h_ref[...]], axis=0), z)
    y = in_turn(c_ref[0], y)
    gram = fold(gram)
    for i in range(out_ref.shape[0]):
        out_ref[i, :R] = y
        out_ref[i, R:] = gram


def last_body(c_ref, z_ref, a_ref, b_ref, o_ref, p_ref, out_ref):
    core = c_ref[0]
    tiles = a_ref.shape[1] // LANES
    near = o_ref.shape[1] // LANES
    far = z_ref.shape[0]
    piece = R // far
    per = z_ref.shape[1] - near * piece
    z = gathered(z_ref, tiles, per)
    rights, gram = against(jnp.concatenate([a_ref[...], b_ref[...]], axis=0), z)

    def feature(i, j):
        return z_ref[i, per + j * piece : per + (j + 1) * piece]

    by_y = [jnp.concatenate([feature(e, q) for e in range(far)], axis=0) for q in range(near)]
    by_z = [jnp.concatenate([feature(q, e) for e in range(far)], axis=0) for q in range(near)]
    feats = jnp.where(core == 0, jnp.concatenate(by_y, axis=1), jnp.concatenate(by_z, axis=1))
    lefts, _ = against(jnp.concatenate([o_ref[...], p_ref[...]], axis=0), feats)
    gram = fold(gram)
    n = out_ref.shape[0] // 2
    mine = jnp.concatenate([lefts[:, :R], rights[:, :R]], axis=1)
    other = jnp.concatenate([lefts[:, R:], rights[:, R:]], axis=1)
    for c in range(2):
        tokens = jnp.where(core == c, mine, other)
        for i in range(n):
            out_ref[c * n + i, :R] = tokens
            out_ref[c * n + i, R:] = gram


def left_body(per, tiles, c_ref, z_ref, yt_ref, inv_ref, left_ref, rows_ref):
    factor(unfold(lines_of(z_ref, tiles * R, H, per)), rows_ref)
    inv = inverse_of(rows_ref)
    inv_ref[...] = inv
    left = nn(inv, yt_ref[...])
    left_ref[...] = jnp.where(c_ref[0] == 0, left[:, :R], left[:, R:]).T


def finish_body(per, c_ref, got_ref, inv_ref, z_ref, w_ref, right_ref, scores_ref, rows_ref):
    s = total_of(got_ref)
    prior = inv_ref[...]
    factor(nt(nn(prior, unfold(s[R:])), prior), rows_ref)
    inv = inverse_of(rows_ref)
    tokens = nn(prior, s[:R])
    mixed = nn(lower_t_of(rows_ref), tokens[:, :R])
    token_right = nn(inv, tokens[:, R:])
    scores_ref[...] = jnp.sum(mixed * token_right, axis=0, keepdims=True)
    whole = nn(inv, prior)
    core = c_ref[0]
    n = right_ref.shape[1]
    tiles = -(-n // (2 * LANES))
    width = tiles * LANES
    mine, other = gathered(z_ref, tiles, per), gathered(w_ref, tiles, per)
    right_ref[:, :width] = product(whole, jnp.where(core == 0, mine, other))
    right_ref[:, width:] = product(whole, jnp.where(core == 0, other, mine))[:, : n - width]


def exchanged(a, axes, groups=None):
    return lax.all_to_all(
        a, axes, split_axis=0, concat_axis=0, tiled=True, axis_index_groups=groups
    )


def lanes_of_chips(far, near):
    def along_y(c):
        return [[(y * near + z) * 2 + c for y in range(far)] for z in range(near)]

    def along_z(c):
        return [[(y * near + z) * 2 + c for z in range(near)] for y in range(far)]

    return along_y(0) + along_z(1), along_z(0) + along_y(1)


def per_device(gradient, start_block, activations, out_grads):
    far, near = lax.axis_size("y"), lax.axis_size("z")
    cols = lax.axis_size("x")
    peers = 2 * cols
    core_at = lax.axis_index("c")
    core = core_at.astype(jnp.int32).reshape(1)
    n = gradient.shape[1]
    width = -(-n // (2 * LANES)) * LANES
    piece = R // peers

    lines = gradient.shape[0]
    first, g, send = call(
        first_body, (shape(peers, H, LANES), shape(lines, width), shape(lines, width)), 3, scalars=1
    )(core, gradient, start_block.T)
    h = other_core(send)
    got = exchanged(first, PEERS)
    a, b = swapped(core, activations, width)
    o, p = swapped(core, out_grads, out_grads.shape[1] // 2)
    square = [pltpu.VMEM((R, LANES), F32)]
    tiles = width // LANES
    each = -(-(tiles * R + H) // (far * near))
    each += -each % (8 // near if near < 8 else 1)
    per = near * each
    first, second = lanes_of_chips(far, near)
    flat = shape(far * per, LANES)
    whole = shape(peers, R + H, LANES)

    def summed(parts, *beside):
        arrived = exchanged(parts.reshape(far, per, LANES), ROWS, first)
        arrived, *beside = lax.optimization_barrier((arrived, *beside))
        cut = call(cut_body, shape(near, each, LANES), 1)(arrived)
        return exchanged(cut, ROWS, second), *beside

    def spread_out(parts, more):
        got = exchanged(parts, ROWS, second)
        body = functools.partial(joined_body, each)
        return exchanged(call(body, shape(far, per + more, LANES), 1)(got), ROWS, first)

    parts = call(spread_first_body, flat, 4, scalars=1)(core, got, g, h)
    arrived, a, b, o, p = summed(parts, a, b, o, p)
    z = spread_out(call(total_body, shape(near, each, LANES), 1)(arrived), 0)
    partial = call(back_body, whole, 4, scalars=1, scratch=square)(core, z, g, h)

    got = exchanged(partial, PEERS)
    parts, yt = call(
        spread_body, (flat, shape(R, LANES)), 4, scalars=1, scratch=square
    )(core, got, g, h)
    eighth = lax.axis_index("x") * 2 + core_at
    mine = lax.dynamic_slice_in_dim(yt, eighth * piece, piece, 0)
    moves = []
    for ys in range(far):
        for cs in range(2):
            for xs in range(cols):
                source = (ys * 2 + cs) * cols + xs
                target = ((2 * xs + cs) * 2 + ys % 2) * cols + ys // 2
                moves.append((source, target))
    lines = lax.ppermute(mine, ("y", "c", "x"), moves)
    arrived, lines = summed(parts, lines)
    sums = call(total_with_body, shape(near, each + piece, LANES), 2)(arrived, lines)
    z = spread_out(sums, near * piece)
    w = other_core(z)
    partial = call(last_body, whole, 6, scalars=1)(core, z, a, b, o, p)
    got = exchanged(partial, PEERS)
    inv, left = call(
        functools.partial(left_body, per, tiles),
        (shape(R, R), shape(R, R)),
        3,
        scalars=1,
        scratch=square,
    )(core, z, yt)
    right, scores = call(
        functools.partial(finish_body, per),
        (shape(R, n), shape(1, R)),
        5,
        scalars=1,
        scratch=square,
    )(core, got, inv, z, w)
    return (left, right.T, scores.reshape(-1))


def solution(mesh):
    sizes = (8, 8, 2, mesh.shape["cols"])
    torus = Mesh(mesh.devices.reshape(sizes), ("y", "z", "c", "x"))
    placed = (P(ROWS, "x"), P("x", None), P(ROWS, "x"), P(ROWS, "x"))
    return jax.shard_map(
        per_device,
        mesh=torus,
        in_specs=placed,
        out_specs=(P(ROWS, None), P("x", None), P(ROWS)),
        check_vma=False,
    )
```

```python
import functools

import jax
import jax.numpy as jnp
from jax import lax
from jax.experimental import pallas as pl
from jax.experimental.pallas import tpu as pltpu
from jax.sharding import Mesh
from jax.sharding import PartitionSpec as P

R = 64
H = R // 2
LANES = 128
F32 = jnp.float32
ROWS = ("y", "z", "c")
CHIPS = ("y", "z")
PEERS = ("c", "x")
HIGH = lax.Precision.HIGHEST

VMEM = pl.BlockSpec(memory_space=pltpu.VMEM)
SMEM = pl.BlockSpec(memory_space=pltpu.SMEM)


def nn(a, b):
    return lax.dot_general(a, b, (((1,), (0,)), ((), ())), precision=HIGH, preferred_element_type=F32)


def nt(a, b):
    return lax.dot_general(a, b, (((1,), (1,)), ((), ())), precision=HIGH, preferred_element_type=F32)


def split(a):
    high = a.astype(jnp.bfloat16)
    rest = a - high.astype(F32)
    middle = rest.astype(jnp.bfloat16)
    return high, middle, (rest - middle.astype(F32)).astype(jnp.bfloat16)


def dot(a, b, dims):
    return lax.dot_general(a, b, (dims, ((), ())), preferred_element_type=F32)


def product(a, b):
    n = a.shape[0]
    lines = jnp.concatenate(split(a), axis=0)
    high, middle, low = split(b)
    dims = ((1,), (0,))
    one = dot(lines, high, dims)
    two = dot(lines[: 2 * n], middle, dims)
    three = dot(lines[:n], low, dims)
    return one[:n] + (one[n : 2 * n] + two[:n] + (one[2 * n :] + two[n:] + three))


def against(lines, z):
    parts = split(z)
    blocks = [*split(lines), *parts]
    n = lines.shape[0]
    out = dot(jnp.concatenate(blocks, axis=0), jnp.concatenate(parts, axis=0), ((1,), (1,)))

    def total(start, length):
        def block(i, j):
            top = start + i * length
            return out[top : top + length, j * R : (j + 1) * R]

        small = block(1, 1) + block(0, 2) + block(2, 0)
        return block(0, 0) + (block(0, 1) + block(1, 0) + small)

    return total(0, n).T, total(3 * n, R)


def call(body, out_shape, n_in, scalars=0, scratch=()):
    specs = [SMEM] * scalars + [VMEM] * (n_in - scalars)
    outs = jax.tree.map(lambda _: VMEM, out_shape)
    return pl.pallas_call(
        body,
        out_shape=out_shape,
        in_specs=specs,
        out_specs=outs,
        scratch_shapes=list(scratch),
        compiler_params=pltpu.CompilerParams(vmem_limit_bytes=48 * 2**20),
    )


def shape(*dims):
    return jax.ShapeDtypeStruct(dims, F32)


def fold(square):
    return jnp.concatenate([square[:H], square[H:]], axis=1)


def unfold(half):
    return jnp.concatenate([half[:, :R], half[:, R:]], axis=0)


def factor(gram, rows_ref):
    b = 8
    line = lax.broadcasted_iota(jnp.int32, (R, R), 0)
    lane = lax.broadcasted_iota(jnp.int32, (R, R), 1)
    both = jnp.concatenate([gram, (line == lane).astype(F32)], axis=1)
    groups = [both[8 * g : 8 * g + 8] for g in range(R // 8)]
    sub = lax.broadcasted_iota(jnp.int32, (8, LANES), 0)
    for k in range(0, R, b):
        g0, off = divmod(k, 8)
        rows = [jnp.broadcast_to(groups[g0][off + i : off + i + 1], (8, LANES)) for i in range(b)]
        live = range(g0 if off + b < 8 else g0 + 1, R // 8)
        cols = {
            g: [jnp.broadcast_to(groups[g][:, k + j : k + j + 1], (8, LANES)) for j in range(b)]
            for g in live
        }
        low = [[None] * b for _ in range(b)]
        inv = [None] * b
        for i in range(b):
            splat = [jnp.broadcast_to(rows[i][:, k + j : k + j + 1], (8, LANES)) for j in range(i + 1)]
            for j in range(i):
                s = splat[j]
                for q in range(j):
                    s = s - low[i][q] * low[j][q]
                low[i][j] = s * inv[j]
            d = splat[i]
            for q in range(i):
                d = d - low[i][q] * low[i][q]
            inv[i] = lax.rsqrt(d)

        def solved(lines):
            done = []
            for i in range(b):
                s = lines[i]
                for q in range(i):
                    s = s - low[i][q] * done[q]
                done.append(s * inv[i])
            return done

        new_rows = solved(rows)
        for i in range(b):
            rows_ref[k + i : k + i + 1, :] = new_rows[i][0:1]
        for g in live:
            f = solved(cols[g])
            upd = f[0] * new_rows[0]
            for i in range(1, b):
                upd = upd + f[i] * new_rows[i]
            if g == g0:
                upd = jnp.where(sub >= off + b, upd, 0.0)
            groups[g] = groups[g] - upd


def inverse_of(rows_ref):
    line = lax.broadcasted_iota(jnp.int32, (R, R), 0)
    lane = lax.broadcasted_iota(jnp.int32, (R, R), 1)
    return jnp.where(line >= lane, rows_ref[:, R:], 0.0)


def lower_t_of(rows_ref):
    line = lax.broadcasted_iota(jnp.int32, (R, R), 0)
    lane = lax.broadcasted_iota(jnp.int32, (R, R), 1)
    return jnp.where(line <= lane, rows_ref[:, :R], 0.0)


def halves(core, a_ref, keep_ref, send_ref):
    width = keep_ref.shape[1]
    rest = a_ref.shape[1] - width

    @pl.when(core == 0)
    def _():
        keep_ref[...] = a_ref[:, :width]
        send_ref[:, :rest] = a_ref[:, width:]
        if rest < width:
            send_ref[:, rest:] = jnp.zeros((send_ref.shape[0], width - rest), F32)

    @pl.when(core != 0)
    def _():
        send_ref[...] = a_ref[:, :width]
        keep_ref[:, :rest] = a_ref[:, width:]
        if rest < width:
            keep_ref[:, rest:] = jnp.zeros((send_ref.shape[0], width - rest), F32)


def halves_body(c_ref, a_ref, keep_ref, send_ref):
    halves(c_ref[0], a_ref, keep_ref, send_ref)


def swapped(core, a, width):
    lines = a.shape[0]
    keep, send = call(halves_body, (shape(lines, width), shape(lines, width)), 2, scalars=1)(core, a)
    return keep, other_core(send)


def other_core(a):
    return lax.ppermute(a, "c", [(0, 1), (1, 0)])


def first_body(c_ref, g_ref, o_ref, out_ref, keep_ref, send_ref):
    y = fold(against(g_ref[...], o_ref[...])[0])
    for i in range(out_ref.shape[0]):
        out_ref[i] = y
    halves(c_ref[0], g_ref, keep_ref, send_ref)


def put_lines(yt, gram, g_refs, core, out_ref):
    lines = jnp.concatenate([g_refs[0][...], g_refs[1][...]], axis=0)
    z = product(in_turn(core, yt), lines)
    tiles = z.shape[1] // LANES
    for t in range(tiles):
        out_ref[t * R : (t + 1) * R] = z[:, t * LANES : (t + 1) * LANES]
    out_ref[tiles * R : tiles * R + H] = fold(gram)
    rest = out_ref.shape[0] - tiles * R - H
    if rest:
        out_ref[tiles * R + H :] = jnp.zeros((rest, LANES), F32)


def spread_first_body(c_ref, got_ref, g_ref, h_ref, out_ref):
    n = got_ref.shape[0] // 2
    parts = []
    for c in range(2):
        s = got_ref[c * n]
        for i in range(1, n):
            s = s + got_ref[c * n + i]
        parts.append(unfold(s))
    yt = jnp.concatenate(parts, axis=1)
    put_lines(yt, nt(yt, yt), (g_ref, h_ref), c_ref[0], out_ref)


def spread_body(c_ref, got_ref, g_ref, h_ref, out_ref, yt_ref, rows_ref):
    s = total_of(got_ref)
    factor(unfold(s[R:]), rows_ref)
    yt = nn(inverse_of(rows_ref), s[:R])
    yt_ref[...] = yt
    put_lines(yt, nt(yt, yt), (g_ref, h_ref), c_ref[0], out_ref)


def total_of(got_ref):
    s = got_ref[0]
    for i in range(1, got_ref.shape[0]):
        s = s + got_ref[i]
    return s


def total_body(got_ref, out_ref):
    s = total_of(got_ref)
    for i in range(out_ref.shape[0]):
        out_ref[i] = s


def total_with_body(got_ref, more_ref, out_ref):
    s = total_of(got_ref)
    n = s.shape[0]
    more = more_ref[...]
    for i in range(out_ref.shape[0]):
        out_ref[i, :n] = s
        out_ref[i, n:] = more


def joined_body(lines, got_ref, out_ref):
    n = got_ref.shape[0]
    s = got_ref[0, :lines]
    for i in range(1, n):
        s = s + got_ref[i, :lines]
    tails = [got_ref[i, lines:] for i in range(n) if got_ref.shape[1] > lines]
    s = jnp.concatenate([s] + tails, axis=0)
    for i in range(out_ref.shape[0]):
        out_ref[i] = s


def lines_of(z_ref, start, length, per):
    parts = []
    while length:
        i, at = divmod(start, per)
        n = min(length, per - at)
        parts.append(z_ref[i, at : at + n])
        start, length = start + n, length - n
    return jnp.concatenate(parts, axis=0) if len(parts) > 1 else parts[0]


def gathered(z_ref, tiles, per):
    return jnp.concatenate([lines_of(z_ref, t * R, R, per) for t in range(tiles)], axis=1)


def in_turn(core, pair):
    turned = jnp.concatenate([pair[:, R:], pair[:, :R]], axis=1)
    return jnp.where(core == 0, pair, turned)


def back_body(c_ref, z_ref, g_ref, h_ref, out_ref, rows_ref):
    tiles = g_ref.shape[1] // LANES
    per = z_ref.shape[1]
    factor(unfold(lines_of(z_ref, tiles * R, H, per)), rows_ref)
    z = product(inverse_of(rows_ref), gathered(z_ref, tiles, per))
    y, gram = against(jnp.concatenate([g_ref[...], h_ref[...]], axis=0), z)
    y = in_turn(c_ref[0], y)
    gram = fold(gram)
    for i in range(out_ref.shape[0]):
        out_ref[i, :R] = y
        out_ref[i, R:] = gram


def last_body(c_ref, z_ref, a_ref, b_ref, o_ref, p_ref, out_ref):
    core = c_ref[0]
    tiles = a_ref.shape[1] // LANES
    near = o_ref.shape[1] // LANES
    far = z_ref.shape[0]
    piece = R // far
    per = z_ref.shape[1] - near * piece
    z = gathered(z_ref, tiles, per)
    rights, gram = against(jnp.concatenate([a_ref[...], b_ref[...]], axis=0), z)

    def feature(i, j):
        return z_ref[i, per + j * piece : per + (j + 1) * piece]

    by_y = [jnp.concatenate([feature(e, q) for e in range(far)], axis=0) for q in range(near)]
    by_z = [jnp.concatenate([feature(q, e) for e in range(far)], axis=0) for q in range(near)]
    feats = jnp.where(core == 0, jnp.concatenate(by_y, axis=1), jnp.concatenate(by_z, axis=1))
    lefts, _ = against(jnp.concatenate([o_ref[...], p_ref[...]], axis=0), feats)
    gram = fold(gram)
    n = out_ref.shape[0] // 2
    mine = jnp.concatenate([lefts[:, :R], rights[:, :R]], axis=1)
    other = jnp.concatenate([lefts[:, R:], rights[:, R:]], axis=1)
    for c in range(2):
        tokens = jnp.where(core == c, mine, other)
        for i in range(n):
            out_ref[c * n + i, :R] = tokens
            out_ref[c * n + i, R:] = gram


def left_body(per, tiles, c_ref, z_ref, yt_ref, inv_ref, left_ref, rows_ref):
    factor(unfold(lines_of(z_ref, tiles * R, H, per)), rows_ref)
    inv = inverse_of(rows_ref)
    inv_ref[...] = inv
    left = nn(inv, yt_ref[...])
    left_ref[...] = jnp.where(c_ref[0] == 0, left[:, :R], left[:, R:]).T


def finish_body(per, c_ref, got_ref, inv_ref, z_ref, w_ref, right_ref, scores_ref, rows_ref):
    s = total_of(got_ref)
    prior = inv_ref[...]
    factor(nt(nn(prior, unfold(s[R:])), prior), rows_ref)
    inv = inverse_of(rows_ref)
    tokens = nn(prior, s[:R])
    mixed = nn(lower_t_of(rows_ref), tokens[:, :R])
    token_right = nn(inv, tokens[:, R:])
    scores_ref[...] = jnp.sum(mixed * token_right, axis=0, keepdims=True)
    whole = nn(inv, prior)
    core = c_ref[0]
    n = right_ref.shape[1]
    tiles = -(-n // (2 * LANES))
    width = tiles * LANES
    mine, other = gathered(z_ref, tiles, per), gathered(w_ref, tiles, per)
    right_ref[:, :width] = product(whole, jnp.where(core == 0, mine, other))
    right_ref[:, width:] = product(whole, jnp.where(core == 0, other, mine))[:, : n - width]


def exchanged(a, axes, groups=None):
    return lax.all_to_all(
        a, axes, split_axis=0, concat_axis=0, tiled=True, axis_index_groups=groups
    )


def lanes_of_chips(far, near):
    def along_y(c):
        return [[(y * near + z) * 2 + c for y in range(far)] for z in range(near)]

    def along_z(c):
        return [[(y * near + z) * 2 + c for z in range(near)] for y in range(far)]

    return along_y(0) + along_z(1), along_z(0) + along_y(1)


def per_device(gradient, start_block, activations, out_grads):
    far, near = lax.axis_size("y"), lax.axis_size("z")
    cols = lax.axis_size("x")
    peers = 2 * cols
    core_at = lax.axis_index("c")
    core = core_at.astype(jnp.int32).reshape(1)
    n = gradient.shape[1]
    width = -(-n // (2 * LANES)) * LANES
    piece = R // peers

    lines = gradient.shape[0]
    first, g, send = call(
        first_body, (shape(peers, H, LANES), shape(lines, width), shape(lines, width)), 3, scalars=1
    )(core, gradient, start_block.T)
    h = other_core(send)
    got = exchanged(first, PEERS)
    a, b = swapped(core, activations, width)
    o, p = swapped(core, out_grads, out_grads.shape[1] // 2)
    square = [pltpu.VMEM((R, LANES), F32)]
    tiles = width // LANES
    per = -(-(tiles * R + H) // (8 * far)) * 8
    first, second = lanes_of_chips(far, near)
    flat = shape(far * per, LANES)
    whole = shape(peers, R + H, LANES)

    def summed(parts, *beside):
        arrived = exchanged(parts.reshape(far, per, LANES), ROWS, first)
        return lax.optimization_barrier((arrived, *beside))

    def spread_out(parts, more):
        got = exchanged(parts, ROWS, second)
        body = functools.partial(joined_body, per)
        return exchanged(call(body, shape(far, per + near * more, LANES), 1)(got), ROWS, first)

    parts = call(spread_first_body, flat, 4, scalars=1)(core, got, g, h)
    arrived, a, b, o, p = summed(parts, a, b, o, p)
    z = spread_out(call(total_body, shape(near, per, LANES), 1)(arrived), 0)
    partial = call(back_body, whole, 4, scalars=1, scratch=square)(core, z, g, h)

    got = exchanged(partial, PEERS)
    parts, yt = call(
        spread_body, (flat, shape(R, LANES)), 4, scalars=1, scratch=square
    )(core, got, g, h)
    eighth = lax.axis_index("x") * 2 + core_at
    mine = lax.dynamic_slice_in_dim(yt, eighth * piece, piece, 0)
    moves = []
    for ys in range(far):
        for cs in range(2):
            for xs in range(cols):
                source = (ys * 2 + cs) * cols + xs
                target = ((2 * xs + cs) * 2 + ys % 2) * cols + ys // 2
                moves.append((source, target))
    lines = lax.ppermute(mine, ("y", "c", "x"), moves)
    arrived, lines = summed(parts, lines)
    sums = call(total_with_body, shape(near, per + piece, LANES), 2)(arrived, lines)
    z = spread_out(sums, piece)
    w = other_core(z)
    partial = call(last_body, whole, 6, scalars=1)(core, z, a, b, o, p)
    got = exchanged(partial, PEERS)
    inv, left = call(
        functools.partial(left_body, per, tiles),
        (shape(R, R), shape(R, R)),
        3,
        scalars=1,
        scratch=square,
    )(core, z, yt)
    right, scores = call(
        functools.partial(finish_body, per),
        (shape(R, n), shape(1, R)),
        5,
        scalars=1,
        scratch=square,
    )(core, got, inv, z, w)
    return (left, right.T, scores.reshape(-1))


def solution(mesh):
    sizes = (8, 8, 2, mesh.shape["cols"])
    torus = Mesh(mesh.devices.reshape(sizes), ("y", "z", "c", "x"))
    placed = (P(ROWS, "x"), P("x", None), P(ROWS, "x"), P(ROWS, "x"))
    return jax.shard_map(
        per_device,
        mesh=torus,
        in_specs=placed,
        out_specs=(P(ROWS, None), P("x", None), P(ROWS)),
        check_vma=False,
    )
```

```python
import functools

import jax
import jax.numpy as jnp
from jax import lax
from jax.experimental import pallas as pl
from jax.experimental.pallas import tpu as pltpu
from jax.sharding import Mesh
from jax.sharding import PartitionSpec as P

R = 64
H = R // 2
LANES = 128
F32 = jnp.float32
ROWS = ("y", "z", "c")
CHIPS = ("y", "z")
PEERS = ("c", "x")
HIGH = lax.Precision.HIGHEST

VMEM = pl.BlockSpec(memory_space=pltpu.VMEM)
SMEM = pl.BlockSpec(memory_space=pltpu.SMEM)


def nn(a, b):
    return lax.dot_general(a, b, (((1,), (0,)), ((), ())), precision=HIGH, preferred_element_type=F32)


def nt(a, b):
    return lax.dot_general(a, b, (((1,), (1,)), ((), ())), precision=HIGH, preferred_element_type=F32)


def split(a):
    high = a.astype(jnp.bfloat16)
    rest = a - high.astype(F32)
    middle = rest.astype(jnp.bfloat16)
    return high, middle, (rest - middle.astype(F32)).astype(jnp.bfloat16)


def dot(a, b, dims):
    return lax.dot_general(a, b, (dims, ((), ())), preferred_element_type=F32)


def product(a, b):
    n = a.shape[0]
    lines = jnp.concatenate(split(a), axis=0)
    high, middle, low = split(b)
    dims = ((1,), (0,))
    one = dot(lines, high, dims)
    two = dot(lines[: 2 * n], middle, dims)
    three = dot(lines[:n], low, dims)
    return one[:n] + (one[n : 2 * n] + two[:n] + (one[2 * n :] + two[n:] + three))


def against(lines, z):
    parts = split(z)
    blocks = [*split(lines), *parts]
    n = lines.shape[0]
    out = dot(jnp.concatenate(blocks, axis=0), jnp.concatenate(parts, axis=0), ((1,), (1,)))

    def total(start, length):
        def block(i, j):
            top = start + i * length
            return out[top : top + length, j * R : (j + 1) * R]

        small = block(1, 1) + block(0, 2) + block(2, 0)
        return block(0, 0) + (block(0, 1) + block(1, 0) + small)

    return total(0, n).T, total(3 * n, R)


def call(body, out_shape, n_in, scalars=0, scratch=()):
    specs = [SMEM] * scalars + [VMEM] * (n_in - scalars)
    outs = jax.tree.map(lambda _: VMEM, out_shape)
    return pl.pallas_call(
        body,
        out_shape=out_shape,
        in_specs=specs,
        out_specs=outs,
        scratch_shapes=list(scratch),
        compiler_params=pltpu.CompilerParams(vmem_limit_bytes=48 * 2**20),
    )


def shape(*dims):
    return jax.ShapeDtypeStruct(dims, F32)


def fold(square):
    return jnp.concatenate([square[:H], square[H:]], axis=1)


def unfold(half):
    return jnp.concatenate([half[:, :R], half[:, R:]], axis=0)


def factor(gram, rows_ref):
    b = 8
    line = lax.broadcasted_iota(jnp.int32, (R, R), 0)
    lane = lax.broadcasted_iota(jnp.int32, (R, R), 1)
    both = jnp.concatenate([gram, (line == lane).astype(F32)], axis=1)
    groups = [both[8 * g : 8 * g + 8] for g in range(R // 8)]
    sub = lax.broadcasted_iota(jnp.int32, (8, LANES), 0)
    for k in range(0, R, b):
        g0, off = divmod(k, 8)
        rows = [jnp.broadcast_to(groups[g0][off + i : off + i + 1], (8, LANES)) for i in range(b)]
        live = range(g0 if off + b < 8 else g0 + 1, R // 8)
        cols = {
            g: [jnp.broadcast_to(groups[g][:, k + j : k + j + 1], (8, LANES)) for j in range(b)]
            for g in live
        }
        low = [[None] * b for _ in range(b)]
        inv = [None] * b
        for i in range(b):
            splat = [jnp.broadcast_to(rows[i][:, k + j : k + j + 1], (8, LANES)) for j in range(i + 1)]
            for j in range(i):
                s = splat[j]
                for q in range(j):
                    s = s - low[i][q] * low[j][q]
                low[i][j] = s * inv[j]
            d = splat[i]
            for q in range(i):
                d = d - low[i][q] * low[i][q]
            inv[i] = lax.rsqrt(d)

        def solved(lines):
            done = []
            for i in range(b):
                s = lines[i]
                for q in range(i):
                    s = s - low[i][q] * done[q]
                done.append(s * inv[i])
            return done

        new_rows = solved(rows)
        for i in range(b):
            rows_ref[k + i : k + i + 1, :] = new_rows[i][0:1]
        for g in live:
            f = solved(cols[g])
            upd = f[0] * new_rows[0]
            for i in range(1, b):
                upd = upd + f[i] * new_rows[i]
            if g == g0:
                upd = jnp.where(sub >= off + b, upd, 0.0)
            groups[g] = groups[g] - upd


def inverse_of(rows_ref):
    line = lax.broadcasted_iota(jnp.int32, (R, R), 0)
    lane = lax.broadcasted_iota(jnp.int32, (R, R), 1)
    return jnp.where(line >= lane, rows_ref[:, R:], 0.0)


def lower_t_of(rows_ref):
    line = lax.broadcasted_iota(jnp.int32, (R, R), 0)
    lane = lax.broadcasted_iota(jnp.int32, (R, R), 1)
    return jnp.where(line <= lane, rows_ref[:, :R], 0.0)


def halves(core, a_ref, keep_ref, send_ref):
    width = keep_ref.shape[1]
    rest = a_ref.shape[1] - width

    @pl.when(core == 0)
    def _():
        keep_ref[...] = a_ref[:, :width]
        send_ref[:, :rest] = a_ref[:, width:]
        if rest < width:
            send_ref[:, rest:] = jnp.zeros((send_ref.shape[0], width - rest), F32)

    @pl.when(core != 0)
    def _():
        send_ref[...] = a_ref[:, :width]
        keep_ref[:, :rest] = a_ref[:, width:]
        if rest < width:
            keep_ref[:, rest:] = jnp.zeros((send_ref.shape[0], width - rest), F32)


def halves_body(c_ref, a_ref, keep_ref, send_ref):
    halves(c_ref[0], a_ref, keep_ref, send_ref)


def swapped(core, a, width):
    lines = a.shape[0]
    keep, send = call(halves_body, (shape(lines, width), shape(lines, width)), 2, scalars=1)(core, a)
    return keep, other_core(send)


def other_core(a):
    return lax.ppermute(a, "c", [(0, 1), (1, 0)])


def first_body(c_ref, g_ref, o_ref, out_ref, keep_ref, send_ref):
    y = fold(against(g_ref[...], o_ref[...])[0])
    for i in range(out_ref.shape[0]):
        out_ref[i] = y
    halves(c_ref[0], g_ref, keep_ref, send_ref)


def put_lines(yt, gram, g_refs, core, out_ref):
    lines = jnp.concatenate([g_refs[0][...], g_refs[1][...]], axis=0)
    z = product(in_turn(core, yt), lines)
    tiles = z.shape[1] // LANES
    for t in range(tiles):
        out_ref[t * R : (t + 1) * R] = z[:, t * LANES : (t + 1) * LANES]
    out_ref[tiles * R : tiles * R + H] = fold(gram)
    rest = out_ref.shape[0] - tiles * R - H
    if rest:
        out_ref[tiles * R + H :] = jnp.zeros((rest, LANES), F32)


def spread_first_body(c_ref, got_ref, g_ref, h_ref, out_ref):
    n = got_ref.shape[0] // 2
    parts = []
    for c in range(2):
        s = got_ref[c * n]
        for i in range(1, n):
            s = s + got_ref[c * n + i]
        parts.append(unfold(s))
    yt = jnp.concatenate(parts, axis=1)
    put_lines(yt, nt(yt, yt), (g_ref, h_ref), c_ref[0], out_ref)


def spread_body(c_ref, got_ref, g_ref, h_ref, out_ref, yt_ref, rows_ref):
    s = total_of(got_ref)
    factor(unfold(s[R:]), rows_ref)
    yt = nn(inverse_of(rows_ref), s[:R])
    yt_ref[...] = yt
    put_lines(yt, nt(yt, yt), (g_ref, h_ref), c_ref[0], out_ref)


def total_of(got_ref):
    s = got_ref[0]
    for i in range(1, got_ref.shape[0]):
        s = s + got_ref[i]
    return s


def total_body(got_ref, out_ref):
    s = total_of(got_ref)
    for i in range(out_ref.shape[0]):
        out_ref[i] = s


def total_with_body(got_ref, more_ref, out_ref):
    s = total_of(got_ref)
    n = s.shape[0]
    more = more_ref[...]
    for i in range(out_ref.shape[0]):
        out_ref[i, :n] = s
        out_ref[i, n:] = more


def joined_body(lines, got_ref, out_ref):
    n = got_ref.shape[0]
    s = got_ref[0, :lines]
    for i in range(1, n):
        s = s + got_ref[i, :lines]
    tails = [got_ref[i, lines:] for i in range(n) if got_ref.shape[1] > lines]
    s = jnp.concatenate([s] + tails, axis=0)
    for i in range(out_ref.shape[0]):
        out_ref[i] = s


def lines_of(z_ref, start, length, per):
    parts = []
    while length:
        i, at = divmod(start, per)
        n = min(length, per - at)
        parts.append(z_ref[i, at : at + n])
        start, length = start + n, length - n
    return jnp.concatenate(parts, axis=0) if len(parts) > 1 else parts[0]


def gathered(z_ref, tiles, per):
    return jnp.concatenate([lines_of(z_ref, t * R, R, per) for t in range(tiles)], axis=1)


def in_turn(core, pair):
    turned = jnp.concatenate([pair[:, R:], pair[:, :R]], axis=1)
    return jnp.where(core == 0, pair, turned)


def back_body(c_ref, z_ref, g_ref, h_ref, out_ref, rows_ref):
    tiles = g_ref.shape[1] // LANES
    per = z_ref.shape[1]
    factor(unfold(lines_of(z_ref, tiles * R, H, per)), rows_ref)
    z = product(inverse_of(rows_ref), gathered(z_ref, tiles, per))
    y, gram = against(jnp.concatenate([g_ref[...], h_ref[...]], axis=0), z)
    y = in_turn(c_ref[0], y)
    gram = fold(gram)
    for i in range(out_ref.shape[0]):
        out_ref[i, :R] = y
        out_ref[i, R:] = gram


def last_body(c_ref, z_ref, a_ref, b_ref, o_ref, p_ref, out_ref):
    core = c_ref[0]
    tiles = a_ref.shape[1] // LANES
    near = o_ref.shape[1] // LANES
    far = z_ref.shape[0]
    piece = R // far
    per = z_ref.shape[1] - near * piece
    z = gathered(z_ref, tiles, per)
    rights, gram = against(jnp.concatenate([a_ref[...], b_ref[...]], axis=0), z)

    def feature(i, j):
        return z_ref[i, per + j * piece : per + (j + 1) * piece]

    by_y = [jnp.concatenate([feature(e, q) for e in range(far)], axis=0) for q in range(near)]
    by_z = [jnp.concatenate([feature(q, e) for e in range(far)], axis=0) for q in range(near)]
    feats = jnp.where(core == 0, jnp.concatenate(by_y, axis=1), jnp.concatenate(by_z, axis=1))
    lefts, _ = against(jnp.concatenate([o_ref[...], p_ref[...]], axis=0), feats)
    gram = fold(gram)
    n = out_ref.shape[0] // 2
    mine = jnp.concatenate([lefts[:, :R], rights[:, :R]], axis=1)
    other = jnp.concatenate([lefts[:, R:], rights[:, R:]], axis=1)
    for c in range(2):
        tokens = jnp.where(core == c, mine, other)
        for i in range(n):
            out_ref[c * n + i, :R] = tokens
            out_ref[c * n + i, R:] = gram


def left_body(per, tiles, c_ref, z_ref, yt_ref, inv_ref, left_ref, rows_ref):
    factor(unfold(lines_of(z_ref, tiles * R, H, per)), rows_ref)
    inv = inverse_of(rows_ref)
    inv_ref[...] = inv
    left = nn(inv, yt_ref[...])
    left_ref[...] = jnp.where(c_ref[0] == 0, left[:, :R], left[:, R:]).T


def finish_body(per, c_ref, got_ref, inv_ref, z_ref, w_ref, right_ref, scores_ref, rows_ref):
    s = total_of(got_ref)
    prior = inv_ref[...]
    factor(nt(nn(prior, unfold(s[R:])), prior), rows_ref)
    inv = inverse_of(rows_ref)
    tokens = nn(prior, s[:R])
    mixed = nn(lower_t_of(rows_ref), tokens[:, :R])
    token_right = nn(inv, tokens[:, R:])
    scores_ref[...] = jnp.sum(mixed * token_right, axis=0, keepdims=True)
    whole = nn(inv, prior)
    core = c_ref[0]
    n = right_ref.shape[1]
    tiles = -(-n // (2 * LANES))
    width = tiles * LANES
    mine, other = gathered(z_ref, tiles, per), gathered(w_ref, tiles, per)
    right_ref[:, :width] = product(whole, jnp.where(core == 0, mine, other))
    right_ref[:, width:] = product(whole, jnp.where(core == 0, other, mine))[:, : n - width]


def exchanged(a, axes, groups=None):
    return lax.all_to_all(
        a, axes, split_axis=0, concat_axis=0, tiled=True, axis_index_groups=groups
    )


def lanes_of_chips(far, near):
    def along_y(c):
        return [[(y * near + z) * 2 + c for y in range(far)] for z in range(near)]

    def along_z(c):
        return [[(y * near + z) * 2 + c for z in range(near)] for y in range(far)]

    return along_y(0) + along_z(1), along_z(0) + along_y(1)


def per_device(gradient, start_block, activations, out_grads):
    far, near = lax.axis_size("y"), lax.axis_size("z")
    cols = lax.axis_size("x")
    peers = 2 * cols
    core_at = lax.axis_index("c")
    core = core_at.astype(jnp.int32).reshape(1)
    n = gradient.shape[1]
    width = -(-n // (2 * LANES)) * LANES
    piece = R // peers

    lines = gradient.shape[0]
    first, g, send = call(
        first_body, (shape(peers, H, LANES), shape(lines, width), shape(lines, width)), 3, scalars=1
    )(core, gradient, start_block.T)
    h = other_core(send)
    got = exchanged(first, PEERS)
    a, b = swapped(core, activations, width)
    o, p = swapped(core, out_grads, out_grads.shape[1] // 2)
    square = [pltpu.VMEM((R, LANES), F32)]
    tiles = width // LANES
    per = -(-(tiles * R + H) // (8 * far)) * 8
    first, second = lanes_of_chips(far, near)
    flat = shape(far * per, LANES)
    whole = shape(peers, R + H, LANES)

    def summed(parts, *beside):
        arrived = exchanged(parts.reshape(far, per, LANES), ROWS, first)
        return lax.optimization_barrier((arrived, *beside))

    def spread_out(parts, more):
        got = exchanged(parts, ROWS, second)
        body = functools.partial(joined_body, per)
        return exchanged(call(body, shape(far, per + near * more, LANES), 1)(got), ROWS, first)

    parts = call(spread_first_body, flat, 4, scalars=1)(core, got, g, h)
    (arrived,) = summed(parts)
    z = spread_out(call(total_body, shape(near, per, LANES), 1)(arrived), 0)
    partial = call(back_body, whole, 4, scalars=1, scratch=square)(core, z, g, h)

    got = exchanged(partial, PEERS)
    parts, yt = call(
        spread_body, (flat, shape(R, LANES)), 4, scalars=1, scratch=square
    )(core, got, g, h)
    eighth = lax.axis_index("x") * 2 + core_at
    mine = lax.dynamic_slice_in_dim(yt, eighth * piece, piece, 0)
    moves = []
    for ys in range(far):
        for cs in range(2):
            for xs in range(cols):
                source = (ys * 2 + cs) * cols + xs
                target = ((2 * xs + cs) * 2 + ys % 2) * cols + ys // 2
                moves.append((source, target))
    lines = lax.ppermute(mine, ("y", "c", "x"), moves)
    arrived, lines, a, b, o, p = summed(parts, lines, a, b, o, p)
    sums = call(total_with_body, shape(near, per + piece, LANES), 2)(arrived, lines)
    z = spread_out(sums, piece)
    w = other_core(z)
    partial = call(last_body, whole, 6, scalars=1)(core, z, a, b, o, p)
    got = exchanged(partial, PEERS)
    inv, left = call(
        functools.partial(left_body, per, tiles),
        (shape(R, R), shape(R, R)),
        3,
        scalars=1,
        scratch=square,
    )(core, z, yt)
    right, scores = call(
        functools.partial(finish_body, per),
        (shape(R, n), shape(1, R)),
        5,
        scalars=1,
        scratch=square,
    )(core, got, inv, z, w)
    return (left, right.T, scores.reshape(-1))


def solution(mesh):
    sizes = (8, 8, 2, mesh.shape["cols"])
    torus = Mesh(mesh.devices.reshape(sizes), ("y", "z", "c", "x"))
    placed = (P(ROWS, "x"), P("x", None), P(ROWS, "x"), P(ROWS, "x"))
    return jax.shard_map(
        per_device,
        mesh=torus,
        in_specs=placed,
        out_specs=(P(ROWS, None), P("x", None), P(ROWS)),
        check_vma=False,
    )
```
